32 devices in a mesh: row: 4 (over y, x), col: 8 (over z, core).
Axes of the slice: x: 2, y: 2, z: 4, core: 2. Of those that a mesh axis runs over, the one named last changes fastest.
Arguments:
- polarization: bfloat16 [4096, 26624], P('row', 'col'), may hold values from -6 to 6
- metric: bfloat16 [26624, 4096], P('row', 'col'), may hold values from -0.0390625 to 0.0390625
- three_panel: bfloat16 [4096, 64, 256], P('row'), may hold values from -0.125 to 0.125
- three_near: bfloat16 [4096, 64, 256], P('col'), may hold values from -0.0078125 to 0.0078125
- green_function: bfloat16 [256, 256], replicated, may hold values from -0.375 to 0.375
- mask_panel: int32 [64, 8], replicated, may hold values 0 or 1
- mask_near: int32 [64, 8], replicated, may hold values 0 or 1
Outputs:
- screened: bfloat16 [4096, 4096], P('row', 'col')
- contracted: bfloat16 [4096, 64, 256], P('col', None, 'row')
- self_energy: float32 [64, 64], P('row', 'col')
The draws below stay inside these ranges and needn't reach their ends.
All inputs are finite; a program needn't handle non-finite values.
Results may differ from the reference program's by a relative error of at most 0.02.
Values may be sent and summed in bfloat16 or wider, within the bound.
No kernel may reach another device: no remote copies, remote signals or barrier semaphores. Data moves between devices by JAX's collectives and lax.ppermute only.
A program may use at most 320 MiB of HBM per device.

```python
import jax
import jax.numpy as jnp
from jax import lax

NRI = 26624
PR = 4096
QW = 4096
TILE = 64
NL = 256
RB = 64
AB = 32
N_ROW = 4


def set_ends(result, key, smallest, top_value):
    extent = result.shape
    index_at = [jax.random.randint(jax.random.fold_in(key, axis), (), 0, extent[axis]) for axis in range(len(extent))]
    result = result.at[tuple(index_at)].set(smallest)
    longest = extent.index(max(extent))
    index_at[longest] = (index_at[longest] + 1) % extent[longest]
    return result.at[tuple(index_at)].set(top_value)


def steps_of(own_key, shape, shards, low, largest):
    loudness, own = 1.0, jax.random.fold_in(own_key, 6)
    for axis_at, shards_of in shards:
        draws = jnp.exp(jax.random.uniform(jax.random.fold_in(own, axis_at), (shards_of,), jnp.float32, low / len(shards), largest / len(shards)))
        loudness = loudness * jnp.repeat(draws, shape[axis_at] // shards_of).reshape([-1 if axis == axis_at else 1 for axis in range(len(shape))])
    return loudness


def gaussian(rng, extent, width, limit, shards=(), held_as=jnp.bfloat16):
    gain = steps_of(rng, extent, shards, -0.22, 0.18) if shards else 1.0
    result = jax.random.normal(rng, extent, jnp.float32) * width * gain
    return jnp.minimum(jnp.maximum(result, -limit), limit).astype(held_as)


def setup_inputs(seed: int = 0) -> dict:
    streams_of = jax.random.split(jax.random.key(seed), 8)
    return {
        "polarization": gaussian(streams_of[0], (PR, NRI), 1.0, 6.0, ((0, 4), (1, 8))),
        "metric": gaussian(streams_of[1], (NRI, QW), NRI ** -0.5, 0.0390625, ((0, 4), (1, 8))),
        "three_panel": gaussian(streams_of[2], (PR, TILE, NL), (PR // 2) ** -0.5, 0.125, ((0, 4),)),
        "three_near": gaussian(streams_of[3], (QW, TILE, NL), (QW * NL // 2) ** -0.5, 0.0078125, ((0, 8),)),
        "green_function": gaussian(streams_of[4], (NL, NL), NL ** -0.5, 0.375),
        "mask_panel": set_ends((jax.random.randint(streams_of[5], (PR // RB, NL // AB), 0, 2) < 1).astype(jnp.int32), jax.random.fold_in(streams_of[5], 1), 0, 1),
        "mask_near": set_ends((jax.random.randint(streams_of[6], (QW // RB, NL // AB), 0, 2) < 1).astype(jnp.int32), jax.random.fold_in(streams_of[6], 1), 0, 1),
    }


def expand_mask(mask, rows, cols):
    return jnp.repeat(jnp.repeat(mask, rows, axis=0), cols, axis=1)


def reference(polarization, metric, three_panel, three_near, green_function, mask_panel, mask_near):
    screened = jnp.dot(polarization, metric, preferred_element_type=jnp.float32).astype(jnp.bfloat16)
    panel = three_panel * expand_mask(mask_panel, RB, AB).astype(jnp.bfloat16)[:, None, :]
    near = three_near * expand_mask(mask_near, RB, AB).astype(jnp.bfloat16)[:, None, :]
    block_rows = PR // N_ROW
    screened_blocks = screened.reshape(N_ROW, block_rows, QW)
    panel_blocks = panel.reshape(N_ROW, block_rows, TILE * NL)

    def add_block(total, pair):
        screened_block, panel_block = pair
        partial_sum = lax.dot_general(screened_block, panel_block, (((0,), (0,)), ((), ())), preferred_element_type=jnp.float32)
        rounded = lax.optimization_barrier(partial_sum.astype(jnp.bfloat16))
        return total + rounded.astype(jnp.float32), None

    contracted, _ = lax.scan(add_block, jnp.zeros((QW, TILE * NL), jnp.float32), (screened_blocks, panel_blocks))
    contracted = contracted.astype(jnp.bfloat16).reshape(QW, TILE, NL)
    dressed = jnp.dot(near.reshape(QW * TILE, NL), green_function.T, preferred_element_type=jnp.float32)
    dressed = dressed.astype(jnp.bfloat16).reshape(QW, TILE, NL)
    self_energy = -lax.dot_general(contracted, dressed, (((0, 2), (0, 2)), ((), ())), preferred_element_type=jnp.float32)
    return screened, contracted, self_energy
```

```python
import functools

import jax
import jax.numpy as jnp
from jax import lax
from jax.experimental import pallas as pl
from jax.experimental.pallas import tpu as pltpu
from jax.sharding import PartitionSpec as P

CHUNKS = 2
MIB = 1024 * 1024


def swap(value, axis, bit):
    size = lax.axis_size(axis)
    return lax.ppermute(value, axis, [(i, i ^ bit) for i in range(size)])


def bits_below(size):
    found = []
    while size > 1:
        size //= 2
        found.append(size)
    return found


def product_kernel(count, order_ref, *refs):
    out_ref = refs[-1]
    total = jnp.dot(refs[0][...], refs[count][0], preferred_element_type=jnp.float32)
    for e in range(1, count):
        total += jnp.dot(refs[e][...], refs[count + e][0], preferred_element_type=jnp.float32)
    out_ref[...] = total.astype(out_ref.dtype)


def product(pieces, stack, order, dtype):
    count = len(pieces)
    rows, depth = pieces[0].shape
    cols = stack.shape[2]
    block = min(256, rows)

    def stack_map(e, i, order_ref):
        return (order_ref[e], 0, 0)

    in_specs = [pl.BlockSpec((block, depth), lambda i, order_ref: (i, 0)) for _ in range(count)]
    in_specs += [pl.BlockSpec((1, depth, cols), functools.partial(stack_map, e)) for e in range(count)]
    return pl.pallas_call(
        functools.partial(product_kernel, count),
        grid_spec=pltpu.PrefetchScalarGridSpec(
            num_scalar_prefetch=1,
            grid=(rows // block,),
            in_specs=in_specs,
            out_specs=pl.BlockSpec((block, cols), lambda i, order_ref: (i, 0)),
        ),
        out_shape=jax.ShapeDtypeStruct((rows, cols), dtype),
        compiler_params=pltpu.CompilerParams(vmem_limit_bytes=40 * MIB),
        cost_estimate=pl.CostEstimate(
            flops=2 * rows * depth * count * cols,
            bytes_accessed=2 * count * depth * (rows + cols) + 4 * rows * cols,
            transcendentals=0,
        ),
    )(order, *pieces, *([stack] * count))


def per_device(
    polarization, metric, three_panel, three_near, green_function, mask_panel, mask_near
):
    r, c = lax.axis_index("row"), lax.axis_index("col")
    row_count, col_count = lax.axis_size("row"), lax.axis_size("col")
    top_row, top_col = row_count // 2, col_count // 2
    u, v = r // top_row, c // top_col
    r_low, c_low = r % top_row, c % top_col
    panel_rows, depth = polarization.shape
    near_cols = metric.shape[1]
    half = depth // 2
    per_block = metric.shape[0] // depth
    tile, near_l = three_panel.shape[1], three_panel.shape[2]
    share = near_l // row_count
    width = near_cols // CHUNKS
    on_diagonal = u == v

    metric_parts = metric.reshape(per_block, 2, half, near_cols)
    metric_mine = lax.dynamic_index_in_dim(metric_parts, u, 1, keepdims=False)
    metric_other = lax.dynamic_index_in_dim(metric_parts, 1 - u, 1, keepdims=False)
    mine = lax.dynamic_slice_in_dim(polarization, u * half, half, 1)
    other = lax.dynamic_slice_in_dim(polarization, (1 - u) * half, half, 1)

    def gather_low(piece):
        found = {0: piece}
        for bit in bits_below(top_col):
            found.update({e ^ bit: swap(p, "col", bit) for e, p in list(found.items())})
        return [found[e] for e in range(top_col)]

    def metric_chunk(j):
        kept = metric_mine[:, :, j * width : (j + 1) * width]
        arrived = swap(metric_other[:, :, j * width : (j + 1) * width], "row", top_row)
        stay = jnp.where(on_diagonal, kept, arrived)
        leave = jnp.where(on_diagonal, arrived, kept)
        both = jnp.concatenate([stay, swap(leave, "col", top_col)], axis=-1)
        found = {0: both}
        for bit in bits_below(top_row):
            found.update({f ^ bit: swap(p, "row", bit) for f, p in list(found.items())})
        return jnp.concatenate([found[f] for f in range(top_row)], axis=0)

    stacks = [metric_chunk(j) for j in range(CHUNKS)]
    crossed = swap(other, "row", top_row)
    pieces_mine = gather_low(mine)
    pieces_crossed = gather_low(crossed)
    blocks = c_low ^ jnp.arange(top_col, dtype=jnp.int32)
    order = ((blocks // per_block) ^ r_low) * per_block + blocks % per_block

    rb = panel_rows * row_count // mask_panel.shape[0]
    ab = near_l // mask_panel.shape[1]
    row_blocks = panel_rows // rb
    panel_mask = lax.dynamic_slice_in_dim(mask_panel, r * row_blocks, row_blocks, 0)
    panel_mask = jnp.repeat(jnp.repeat(panel_mask, rb, 0), ab, 1).astype(jnp.bfloat16)
    panel = three_panel * panel_mask[:, None, :]
    panel = jnp.transpose(panel, (1, 2, 0))
    shares = [
        lax.dynamic_slice_in_dim(panel, (r ^ e) * share, share, 1).reshape(tile * share, panel_rows)
        for e in range(row_count)
    ]

    near_blocks = near_cols // rb
    near_mask = lax.dynamic_slice_in_dim(mask_near, c * near_blocks, near_blocks, 0)
    near_mask = jnp.repeat(jnp.repeat(near_mask, rb, 0), ab, 1).astype(jnp.bfloat16)
    near = three_near * near_mask[:, None, :]
    green = lax.dynamic_slice_in_dim(green_function, r * share, share, 0)
    dressed = jnp.einsum("qns,ls->nlq", near, green, preferred_element_type=jnp.float32).astype(jnp.bfloat16)

    screened_chunks, contracted_chunks = [], []
    energy = jnp.zeros((tile, tile), jnp.float32)
    for j in range(CHUNKS):
        away = product(pieces_crossed, stacks[j], order, jnp.bfloat16)
        home = product(pieces_mine, stacks[j], order, jnp.float32)
        home = home + swap(away, "row", top_row).astype(jnp.float32)
        arrived = swap(home[:, width:].astype(jnp.bfloat16), "col", top_col)
        screened = (home[:, :width] + arrived.astype(jnp.float32)).astype(jnp.bfloat16)
        screened_chunks.append(screened)

        sums = {}
        for e in reversed(range(row_count)):
            sums[e] = jnp.dot(shares[e], screened, preferred_element_type=jnp.float32).astype(jnp.bfloat16)
        bits = bits_below(row_count)
        bits = bits if j % 2 else bits[::-1]
        for bit in bits:
            gone = [e for e in sums if e & bit]
            arrived = {e ^ bit: swap(sums.pop(e), "row", bit) for e in gone}
            for e, value in arrived.items():
                sums[e] = (sums[e].astype(jnp.float32) + value.astype(jnp.float32)).astype(jnp.bfloat16)
        contracted = sums[0].reshape(tile, share, width)
        contracted_chunks.append(contracted)
        energy = energy - jnp.einsum(
            "mlq,nlq->mn",
            contracted,
            dressed[:, :, j * width : (j + 1) * width],
            preferred_element_type=jnp.float32,
        )

    energy = lax.psum(energy, ("row", "col"))
    rows, cols = tile // row_count, tile // col_count
    energy = lax.dynamic_slice(energy, (r * rows, c * cols), (rows, cols))
    contracted = jnp.transpose(jnp.concatenate(contracted_chunks, axis=2), (2, 0, 1))
    return jnp.concatenate(screened_chunks, axis=1), contracted, energy


def solution(mesh):
    placed = (
        P("row", "col"),
        P("row", "col"),
        P("row", None, None),
        P("col", None, None),
        P(),
        P(),
        P(),
    )
    return jax.shard_map(
        per_device,
        mesh=mesh,
        in_specs=placed,
        out_specs=(P("row", "col"), P("col", None, "row"), P("row", "col")),
        check_vma=False,
    )
```

```python
import functools

import jax
import jax.numpy as jnp
from jax import lax
from jax.experimental import pallas as pl
from jax.experimental.pallas import tpu as pltpu
from jax.sharding import PartitionSpec as P

WIDTH = 128
PAIR = 2
GROUPS = 4
VMEM = 56
MIB = 1024 * 1024


def swap(value, axis, bit):
    size = lax.axis_size(axis)
    return lax.ppermute(value, axis, [(i, i ^ bit) for i in range(size)])


def after(value, *others):
    return lax.optimization_barrier((value, others))[0]


class Link:
    def __init__(self, in_flight):
        self.past, self.in_flight = [], in_flight

    def swap(self, value, axis, bit):
        if len(self.past) >= self.in_flight:
            value = after(value, self.past[-self.in_flight])
        self.past.append(swap(value, axis, bit))
        return self.past[-1]


def bits_below(size):
    found = []
    while size > 1:
        size //= 2
        found.append(size)
    return found


def product_kernel(count, parts, per_block, order_ref, *refs):
    pieces, sources, out_ref = refs[: count * parts], refs[count * parts : -6], refs[-6]
    held, weights, total, piece_sems, weight_sems = refs[-5:]
    width = sources[0].shape[2]
    sides = weights.shape[2] // width
    blocks = range(len(sources) // sides)

    def load(e, side, block):
        return pltpu.make_async_copy(
            sources[sides * block + side].at[order_ref[e] % per_block],
            weights.at[e, :, pl.ds(side * width, width)],
            weight_sems.at[e, side],
        )

    rows = pieces[0].shape[0]
    copies = [
        pltpu.make_async_copy(piece, held.at[i // parts, pl.ds(i % parts * rows, rows)], piece_sems.at[i])
        for i, piece in enumerate(pieces)
    ]
    for e in range(count):
        for side in range(sides):
            for block in blocks:

                @pl.when(order_ref[e] // per_block == block)
                def _():
                    load(e, side, block).start()

        for copy in copies[e * parts : (e + 1) * parts]:
            copy.start()
    for e in range(count):
        for side in range(sides):
            load(e, side, 0).wait()
        for copy in copies[e * parts : (e + 1) * parts]:
            copy.wait()
        part = jnp.dot(held[e], weights[e], preferred_element_type=jnp.float32)
        if e == 0:
            total[...] = part
        elif e < count - 1:
            total[...] += part
        else:
            out_ref[...] = (total[...] + part).astype(out_ref.dtype)


def product(pieces, sources, order, per_block, dtype):
    count, parts = len(pieces), len(pieces[0])
    rows, depth = pieces[0][0].shape
    rows *= parts
    sides = len(sources[0])
    cols = sides * sources[0][0].shape[2]
    sources = [part for block in sources for part in block]
    in_hbm = pl.BlockSpec(memory_space=pl.ANY)
    return pl.pallas_call(
        functools.partial(product_kernel, count, parts, per_block),
        in_specs=[pl.BlockSpec(memory_space=pltpu.SMEM)] + [in_hbm] * (count * parts + len(sources)),
        out_specs=pl.BlockSpec(memory_space=pltpu.VMEM),
        out_shape=jax.ShapeDtypeStruct((rows, cols), dtype),
        scratch_shapes=[
            pltpu.VMEM((count, rows, depth), jnp.bfloat16),
            pltpu.VMEM((count, depth, cols), jnp.bfloat16),
            pltpu.VMEM((rows, cols), jnp.float32),
            pltpu.SemaphoreType.DMA((count * parts,)),
            pltpu.SemaphoreType.DMA((count, sides)),
        ],
        compiler_params=pltpu.CompilerParams(vmem_limit_bytes=VMEM * MIB),
        cost_estimate=pl.CostEstimate(
            flops=2 * rows * depth * count * cols,
            bytes_accessed=2 * count * depth * (rows + cols) + 4 * rows * cols,
            transcendentals=0,
        ),
    )(order, *[part for piece in pieces for part in piece], *sources)


def turn_kernel(panel_ref, out_ref):
    out_ref[...] = jnp.transpose(panel_ref[...], (1, 2, 0))


def turn(panel, first, rows):
    _, tile, near_l = panel.shape
    tall = tile // GROUPS
    wide = min(rows, 128)
    return pl.pallas_call(
        turn_kernel,
        grid=(rows // wide, tile // tall),
        in_specs=[pl.BlockSpec((wide, tall, near_l), lambda i, g: (first // wide + i, g, 0))],
        out_specs=pl.BlockSpec((tall, near_l, wide), lambda i, g: (g, 0, i)),
        out_shape=jax.ShapeDtypeStruct((tile, near_l, rows), panel.dtype),
        compiler_params=pltpu.CompilerParams(vmem_limit_bytes=VMEM * MIB),
        cost_estimate=pl.CostEstimate(flops=0, bytes_accessed=4 * rows * tile * near_l, transcendentals=0),
    )(panel)


def contract_kernel(rb, ab, places_ref, mask_ref, screened_ref, *refs):
    panels, outs, (held, masked, sems) = refs[:-5], refs[-5:-3], refs[-3:]
    _, tall, share, rows = held.shape
    per_share = masked.shape[1]
    each = rows // len(panels)
    count, half = outs[0].shape[:2]
    steps = [(h, i, g) for h in range(2) for i in range(count) for g in range(half // tall)]

    def load(k):
        h, i, g = steps[k]
        at = pl.ds(pl.multiple_of(places_ref[h, i] * share, share), share)
        return [
            pltpu.make_async_copy(
                panel.at[pl.ds(h * half + g * tall, tall), at, :],
                held.at[k % 2, :, :, pl.ds(n * each, each)],
                sems.at[k % 2, n],
            )
            for n, panel in enumerate(panels)
        ]

    for copy in load(0):
        copy.start()
    for k, (h, i, g) in enumerate(steps):
        if k + 1 < len(steps):
            for copy in load(k + 1):
                copy.start()
        if g == 0:
            for b in range(per_share):
                for n in range(rows // rb):
                    part = screened_ref[pl.ds(n * rb, rb), :]
                    flag = mask_ref[n, places_ref[h, i] * per_share + b]
                    masked[i % 2, b, pl.ds(n * rb, rb), :] = jnp.where(flag != 0, part, jnp.zeros_like(part))
        for copy in load(k):
            copy.wait()
        for b in range(per_share):
            block = held[k % 2, :, pl.ds(b * ab, ab), :].reshape(tall * ab, rows)
            part = jnp.dot(block, masked[i % 2, b], preferred_element_type=jnp.float32)
            outs[h][i, pl.ds(g * tall, tall), pl.ds(b * ab, ab), :] = part.astype(outs[h].dtype).reshape(
                tall, ab, part.shape[1]
            )


def contract(panels, screened, mask, places, rb, ab, share):
    count = places.shape[1]
    tile, rows = panels[0].shape[0], screened.shape[0]
    tall = tile // GROUPS
    width = screened.shape[1]
    in_smem, in_hbm = pl.BlockSpec(memory_space=pltpu.SMEM), pl.BlockSpec(memory_space=pl.ANY)
    in_vmem = pl.BlockSpec(memory_space=pltpu.VMEM)
    return pl.pallas_call(
        functools.partial(contract_kernel, rb, ab),
        in_specs=[in_smem, in_smem, in_vmem] + [in_hbm] * len(panels),
        out_specs=[in_vmem] * 2,
        out_shape=[jax.ShapeDtypeStruct((count, tile // 2, share, width), jnp.bfloat16)] * 2,
        scratch_shapes=[
            pltpu.VMEM((2, tall, share, rows), jnp.bfloat16),
            pltpu.VMEM((2, share // ab, rows, width), jnp.bfloat16),
            pltpu.SemaphoreType.DMA((2, len(panels))),
        ],
        compiler_params=pltpu.CompilerParams(vmem_limit_bytes=VMEM * MIB),
        cost_estimate=pl.CostEstimate(
            flops=2 * count * tile * share * rows * width,
            bytes_accessed=2 * count * tile * share * (rows + width),
            transcendentals=0,
        ),
    )(places, mask, screened, *panels)


def scatter_sum(value, axis):
    at = lax.axis_index(axis)
    for bit in bits_below(lax.axis_size(axis)):
        halves = value.reshape(2, value.shape[0] // 2, *value.shape[1:])
        mine = (at // bit) % 2
        value = lax.dynamic_index_in_dim(halves, mine, 0, keepdims=False) + swap(
            lax.dynamic_index_in_dim(halves, 1 - mine, 0, keepdims=False), axis, bit
        )
    return value


def per_device(
    polarization, metric, three_panel, three_near, green_function, mask_panel, mask_near
):
    r, c = lax.axis_index("row"), lax.axis_index("col")
    row_count, col_count = lax.axis_size("row"), lax.axis_size("col")
    top_row, top_col = row_count // 2, col_count // 2
    u, v = r // top_row, c // top_col
    r_low, c_low = r % top_row, c % top_col
    panel_rows, depth = polarization.shape
    near_cols = metric.shape[1]
    half = depth // 2
    per_block = metric.shape[0] // depth
    tile, near_l = three_panel.shape[1], three_panel.shape[2]
    share = near_l // row_count
    width = min(WIDTH, near_cols)
    chunks = near_cols // width
    on_diagonal = u == v

    metric_parts = metric.reshape(per_block, 2, half, near_cols)
    metric_mine = lax.dynamic_index_in_dim(metric_parts, u, 1, keepdims=False)
    metric_other = lax.dynamic_index_in_dim(metric_parts, 1 - u, 1, keepdims=False)
    crossing = [metric_other[:, :, j * width : (j + 1) * width] for j in range(chunks)]
    polarization = after(polarization, crossing[0])
    mine = lax.dynamic_slice_in_dim(polarization, u * half, half, 1)
    other = lax.dynamic_slice_in_dim(polarization, (1 - u) * half, half, 1)

    first, second = jnp.split(mine, 2)
    other_first, other_second = jnp.split(other, 2)
    low = top_col // 2

    def cross(value, *others):
        return swap(after(value, *others), "row", top_row)

    arrived, came = [cross(crossing[0])], []
    near_first = swap(first, "col", low)
    crossed_first = cross(other_first, arrived[0])
    near_second = swap(after(second, near_first, arrived[0]), "col", low)
    panels = []

    def turn_next(*others):
        rows = panel_rows // GROUPS
        panels.append(turn(after(three_panel, *others), len(panels) * rows, rows))
        return panels[-1]

    def far(j, *others):
        kept = after(metric_mine, arrived[j])[:, :, j * width : (j + 1) * width]
        stay = jnp.where(on_diagonal, kept, arrived[j])
        leave = jnp.where(on_diagonal, arrived[j], kept)
        came.append([stay, swap(after(leave, *others), "col", top_col)])

    row_links = {bit: Link(2) for bit in bits_below(top_row)}

    def gather_rows(pair):
        found = {0: pair}
        for bit in bits_below(top_row):
            for f, parts in list(found.items()):
                found[f ^ bit] = [row_links[bit].swap(p, "row", bit) for p in parts]
        return [found[f] for f in range(top_row)]

    far(0)
    gathered = [gather_rows(came[0])]
    arrived.append(cross(crossing[1], arrived[0], near_first))
    crossed_second = cross(other_second, crossed_first)
    far(1, near_first, turn_next(near_first))
    gathered.append(gather_rows(came[1]))
    near_crossed_first = swap(after(crossed_first, near_second, arrived[1], came[0][1]), "col", low)
    turn_next(crossed_first, *panels)
    for j in range(2, chunks):
        arrived.append(cross(crossing[j], *([arrived[1], near_second] if j == 2 else [crossed_second])))
        far(j, came[j - 2][1], near_second, gathered[j - 2][-1], turn_next(arrived[j - 1], *panels))
        gathered.append(gather_rows(came[j]))
    near_crossed_second = swap(after(crossed_second, near_crossed_first, arrived[-1], came[1][1]), "col", low)
    while len(panels) < GROUPS:
        turn_next(crossed_second, *panels)

    def gather_low(found):
        link = Link(1)
        for bit in bits_below(low):
            for e, parts in list(found.items()):
                found[e ^ bit] = [link.swap(p, "col", bit) if bit > 1 else swap(p, "col", bit) for p in parts]
        return [found[e] for e in range(top_col)]

    pieces_mine = gather_low({0: [first, second], low: [near_first, near_second]})
    pieces_crossed = gather_low({0: [crossed_first, crossed_second], low: [near_crossed_first, near_crossed_second]})
    blocks = c_low ^ jnp.arange(top_col, dtype=jnp.int32)
    order = ((blocks // per_block) ^ r_low) * per_block + blocks % per_block

    rb = panel_rows * row_count // mask_panel.shape[0]
    ab = near_l // mask_panel.shape[1]
    row_blocks = panel_rows // rb
    panel_mask = lax.dynamic_slice_in_dim(mask_panel, r * row_blocks, row_blocks, 0)

    near_blocks = near_cols // rb
    near_mask = lax.dynamic_slice_in_dim(mask_near, c * near_blocks, near_blocks, 0)
    near_mask = jnp.repeat(jnp.repeat(near_mask, rb, 0), ab, 1).astype(jnp.bfloat16)
    near = after(three_near, near_crossed_first) * near_mask[:, None, :]
    green = lax.dynamic_slice_in_dim(green_function, r * share, share, 0)
    dressed = jnp.einsum("qns,ls->nlq", near, green, preferred_element_type=jnp.float32).astype(jnp.bfloat16)

    earlier = (*panels, dressed)
    screened_chunks, contracted_chunks = [], []
    energy = jnp.zeros((tile, tile), jnp.float32)
    hops = {bit: Link(1) for bit in bits_below(row_count)}
    pair = min(PAIR, chunks)
    wide = pair * width
    orders = [bits_below(row_count)[::-1], bits_below(row_count)]
    kept = [[e for e in range(row_count) if not e & bits[0]] for bits in orders]
    places = r ^ jnp.array(kept, jnp.int32)
    first_bits = jnp.array([[bits[0]] for bits in orders], jnp.int32)
    for j in range(0, chunks, pair):
        sources = [[gathered[j + i][f][side] for side in range(2) for i in range(pair)] for f in range(top_row)]
        away = product(pieces_crossed, sources, after(order, *earlier), per_block, jnp.bfloat16)
        home = product(pieces_mine, sources, after(order, away), per_block, jnp.float32)
        home = home + swap(away, "row", top_row).astype(jnp.float32)
        came_back = swap(home[:, wide:].astype(jnp.bfloat16), "col", top_col)
        screened = (home[:, :wide] + came_back.astype(jnp.float32)).astype(jnp.bfloat16)
        screened_chunks.append(screened)

        gone = list(contract(panels, screened, panel_mask, places ^ first_bits, rb, ab, share))
        stay = list(contract(panels, screened, panel_mask, after(places, gone), rb, ab, share))
        earlier = (home, *gone)
        left, halves = [kept[h] for h in range(2)], []
        for hop in range(len(orders[0])):
            for h, bits in enumerate(orders):
                total = stay[h].astype(jnp.float32) + hops[bits[hop]].swap(gone[h], "row", bits[hop]).astype(jnp.float32)
                total = total.astype(jnp.bfloat16)
                if hop + 1 < len(bits):
                    staying = [e for e in left[h] if not e & bits[hop + 1]]
                    gone[h] = jnp.stack([total[left[h].index(e | bits[hop + 1])] for e in staying])
                    stay[h] = jnp.stack([total[left[h].index(e)] for e in staying])
                    left[h] = staying
                else:
                    halves.append(total[0])
        contracted_chunks.append(jnp.concatenate(halves))
        parts = [
            jnp.einsum("mlq,nlq->mn", half, dressed[:, :, j * width : j * width + wide], preferred_element_type=jnp.float32)
            for half in halves
        ]
        energy = energy - jnp.concatenate(parts)

    energy = scatter_sum(scatter_sum(energy, "row").T, "col").T
    contracted = jnp.transpose(jnp.concatenate(contracted_chunks, axis=2), (2, 0, 1))
    return jnp.concatenate(screened_chunks, axis=1), contracted, energy


def solution(mesh):
    placed = (
        P("row", "col"),
        P("row", "col"),
        P("row", None, None),
        P("col", None, None),
        P(),
        P(),
        P(),
    )
    return jax.shard_map(
        per_device,
        mesh=mesh,
        in_specs=placed,
        out_specs=(P("row", "col"), P("col", None, "row"), P("row", "col")),
        check_vma=False,
    )
```

```python
import functools

import jax
import jax.numpy as jnp
from jax import lax
from jax.experimental import pallas as pl
from jax.experimental.pallas import tpu as pltpu
from jax.sharding import PartitionSpec as P

WIDTH = 128
PAIR = 2
GROUPS = 4
VMEM = 56
MIB = 1024 * 1024


def swap(value, axis, bit):
    size = lax.axis_size(axis)
    return lax.ppermute(value, axis, [(i, i ^ bit) for i in range(size)])


def after(value, *others):
    return lax.optimization_barrier((value, others))[0]


class Link:
    def __init__(self, in_flight):
        self.past, self.in_flight = [], in_flight

    def swap(self, value, axis, bit):
        if len(self.past) >= self.in_flight:
            value = after(value, self.past[-self.in_flight])
        self.past.append(swap(value, axis, bit))
        return self.past[-1]


def bits_below(size):
    found = []
    while size > 1:
        size //= 2
        found.append(size)
    return found


def product_kernel(count, parts, per_block, order_ref, *refs):
    pieces, sources, out_ref = refs[: count * parts], refs[count * parts : -6], refs[-6]
    held, weights, total, piece_sems, weight_sems = refs[-5:]
    width = sources[0].shape[2]
    sides = weights.shape[2] // width
    blocks = range(len(sources) // sides)

    def load(e, side, block):
        return pltpu.make_async_copy(
            sources[sides * block + side].at[order_ref[e] % per_block],
            weights.at[e, :, pl.ds(side * width, width)],
            weight_sems.at[e, side],
        )

    rows = pieces[0].shape[0]
    copies = [
        pltpu.make_async_copy(piece, held.at[i // parts, pl.ds(i % parts * rows, rows)], piece_sems.at[i])
        for i, piece in enumerate(pieces)
    ]
    for e in range(count):
        for side in range(sides):
            for block in blocks:

                @pl.when(order_ref[e] // per_block == block)
                def _():
                    load(e, side, block).start()

        for copy in copies[e * parts : (e + 1) * parts]:
            copy.start()
    for e in range(count):
        for side in range(sides):
            load(e, side, 0).wait()
        for copy in copies[e * parts : (e + 1) * parts]:
            copy.wait()
        part = jnp.dot(held[e], weights[e], preferred_element_type=jnp.float32)
        if e == 0:
            total[...] = part
        elif e < count - 1:
            total[...] += part
        else:
            out_ref[...] = (total[...] + part).astype(out_ref.dtype)


def product(pieces, sources, order, per_block, dtype):
    count, parts = len(pieces), len(pieces[0])
    rows, depth = pieces[0][0].shape
    rows *= parts
    sides = len(sources[0])
    cols = sides * sources[0][0].shape[2]
    sources = [part for block in sources for part in block]
    in_hbm = pl.BlockSpec(memory_space=pl.ANY)
    return pl.pallas_call(
        functools.partial(product_kernel, count, parts, per_block),
        in_specs=[pl.BlockSpec(memory_space=pltpu.SMEM)] + [in_hbm] * (count * parts + len(sources)),
        out_specs=pl.BlockSpec(memory_space=pltpu.VMEM),
        out_shape=jax.ShapeDtypeStruct((rows, cols), dtype),
        scratch_shapes=[
            pltpu.VMEM((count, rows, depth), jnp.bfloat16),
            pltpu.VMEM((count, depth, cols), jnp.bfloat16),
            pltpu.VMEM((rows, cols), jnp.float32),
            pltpu.SemaphoreType.DMA((count * parts,)),
            pltpu.SemaphoreType.DMA((count, sides)),
        ],
        compiler_params=pltpu.CompilerParams(vmem_limit_bytes=VMEM * MIB),
        cost_estimate=pl.CostEstimate(
            flops=2 * rows * depth * count * cols,
            bytes_accessed=2 * count * depth * (rows + cols) + 4 * rows * cols,
            transcendentals=0,
        ),
    )(order, *[part for piece in pieces for part in piece], *sources)


def turn_kernel(panel_ref, out_ref):
    out_ref[...] = jnp.transpose(panel_ref[...], (1, 2, 0))


def turn(panel, first, rows):
    _, tile, near_l = panel.shape
    tall = tile // GROUPS
    wide = min(rows, 128)
    return pl.pallas_call(
        turn_kernel,
        grid=(rows // wide, tile // tall),
        in_specs=[pl.BlockSpec((wide, tall, near_l), lambda i, g: (first // wide + i, g, 0))],
        out_specs=pl.BlockSpec((tall, near_l, wide), lambda i, g: (g, 0, i)),
        out_shape=jax.ShapeDtypeStruct((tile, near_l, rows), panel.dtype),
        compiler_params=pltpu.CompilerParams(vmem_limit_bytes=VMEM * MIB),
        cost_estimate=pl.CostEstimate(flops=0, bytes_accessed=4 * rows * tile * near_l, transcendentals=0),
    )(panel)


def contract_kernel(rb, ab, places_ref, mask_ref, screened_ref, *refs):
    count = places_ref.shape[1]
    held, masked, sems = refs[-3:]
    panels, outs = refs[: -3 - 2 * count], refs[-3 - 2 * count : -3]
    _, tall, share, rows = held.shape
    per_share = masked.shape[1]
    each = rows // len(panels)
    half = outs[0].shape[0]
    steps = [(h, i, g) for h in range(2) for i in range(count) for g in range(half // tall)]

    def load(k):
        h, i, g = steps[k]
        at = pl.ds(pl.multiple_of(places_ref[h, i] * share, share), share)
        return [
            pltpu.make_async_copy(
                panel.at[pl.ds(h * half + g * tall, tall), at, :],
                held.at[k % 2, :, :, pl.ds(n * each, each)],
                sems.at[k % 2, n],
            )
            for n, panel in enumerate(panels)
        ]

    for copy in load(0):
        copy.start()
    for k, (h, i, g) in enumerate(steps):
        if k + 1 < len(steps):
            for copy in load(k + 1):
                copy.start()
        if g == 0:
            for b in range(per_share):
                for n in range(rows // rb):
                    part = screened_ref[pl.ds(n * rb, rb), :]
                    flag = mask_ref[n, places_ref[h, i] * per_share + b]
                    masked[i % 2, b, pl.ds(n * rb, rb), :] = jnp.where(flag != 0, part, jnp.zeros_like(part))
        for copy in load(k):
            copy.wait()
        for b in range(per_share):
            block = held[k % 2, :, pl.ds(b * ab, ab), :].reshape(tall * ab, rows)
            part = jnp.dot(block, masked[i % 2, b], preferred_element_type=jnp.float32)
            outs[h * count + i][pl.ds(g * tall, tall), pl.ds(b * ab, ab), :] = part.astype(outs[0].dtype).reshape(
                tall, ab, part.shape[1]
            )


def contract(panels, screened, mask, places, rb, ab, share):
    count = places.shape[1]
    tile, rows = panels[0].shape[0], screened.shape[0]
    tall = tile // GROUPS
    width = screened.shape[1]
    in_smem, in_hbm = pl.BlockSpec(memory_space=pltpu.SMEM), pl.BlockSpec(memory_space=pl.ANY)
    in_vmem = pl.BlockSpec(memory_space=pltpu.VMEM)
    found = pl.pallas_call(
        functools.partial(contract_kernel, rb, ab),
        in_specs=[in_smem, in_smem, in_vmem] + [in_hbm] * len(panels),
        out_specs=[in_vmem] * (2 * count),
        out_shape=[jax.ShapeDtypeStruct((tile // 2, share, width), jnp.bfloat16)] * (2 * count),
        scratch_shapes=[
            pltpu.VMEM((2, tall, share, rows), jnp.bfloat16),
            pltpu.VMEM((2, share // ab, rows, width), jnp.bfloat16),
            pltpu.SemaphoreType.DMA((2, len(panels))),
        ],
        compiler_params=pltpu.CompilerParams(vmem_limit_bytes=VMEM * MIB),
        cost_estimate=pl.CostEstimate(
            flops=2 * count * tile * share * rows * width,
            bytes_accessed=2 * count * tile * share * (rows + width),
            transcendentals=0,
        ),
    )(places, mask, screened, *panels)
    return [list(found[:count]), list(found[count:])]


def scatter_sum(value, axis):
    at = lax.axis_index(axis)
    for bit in bits_below(lax.axis_size(axis)):
        halves = value.reshape(2, value.shape[0] // 2, *value.shape[1:])
        mine = (at // bit) % 2
        value = lax.dynamic_index_in_dim(halves, mine, 0, keepdims=False) + swap(
            lax.dynamic_index_in_dim(halves, 1 - mine, 0, keepdims=False), axis, bit
        )
    return value


def per_device(
    polarization, metric, three_panel, three_near, green_function, mask_panel, mask_near
):
    r, c = lax.axis_index("row"), lax.axis_index("col")
    row_count, col_count = lax.axis_size("row"), lax.axis_size("col")
    top_row, top_col = row_count // 2, col_count // 2
    u, v = r // top_row, c // top_col
    r_low, c_low = r % top_row, c % top_col
    panel_rows, depth = polarization.shape
    near_cols = metric.shape[1]
    half = depth // 2
    per_block = metric.shape[0] // depth
    tile, near_l = three_panel.shape[1], three_panel.shape[2]
    share = near_l // row_count
    width = min(WIDTH, near_cols)
    chunks = near_cols // width
    on_diagonal = u == v

    metric_parts = metric.reshape(per_block, 2, half, near_cols)
    metric_mine = lax.dynamic_index_in_dim(metric_parts, u, 1, keepdims=False)
    metric_other = lax.dynamic_index_in_dim(metric_parts, 1 - u, 1, keepdims=False)
    crossing = [metric_other[:, :, j * width : (j + 1) * width] for j in range(chunks)]
    polarization = after(polarization, crossing[0])
    mine = lax.dynamic_slice_in_dim(polarization, u * half, half, 1)
    other = lax.dynamic_slice_in_dim(polarization, (1 - u) * half, half, 1)

    first, second = jnp.split(mine, 2)
    other_first, other_second = jnp.split(other, 2)
    low = top_col // 2

    def cross(value, *others):
        return swap(after(value, *others), "row", top_row)

    arrived, came = [cross(crossing[0])], []
    near_first = swap(first, "col", low)
    crossed_first = cross(other_first, arrived[0])
    near_second = swap(after(second, near_first, arrived[0]), "col", low)
    panels = []

    def turn_next(*others):
        rows = panel_rows // GROUPS
        panels.append(turn(after(three_panel, *others), len(panels) * rows, rows))
        return panels[-1]

    def far(j, *others):
        kept = after(metric_mine, arrived[j])[:, :, j * width : (j + 1) * width]
        stay = jnp.where(on_diagonal, kept, arrived[j])
        leave = jnp.where(on_diagonal, arrived[j], kept)
        came.append([stay, swap(after(leave, *others), "col", top_col)])
        return leave

    row_links = {bit: Link(2) for bit in bits_below(top_row)}

    def gather_rows(pair):
        found = {0: pair}
        for bit in bits_below(top_row):
            for f, parts in list(found.items()):
                found[f ^ bit] = [row_links[bit].swap(p, "row", bit) for p in parts]
        return [found[f] for f in range(top_row)]

    row_links = {bit: Link(2) for bit in bits_below(top_row)}
    gathered = []

    def gather_rows(pair):
        found = {0: pair}
        for bit in bits_below(top_row):
            for f, parts in list(found.items()):
                found[f ^ bit] = [row_links[bit].swap(p, "row", bit) for p in parts]
        gathered.append([found[f] for f in range(top_row)])

    def from_row(j, side):
        return gathered[j][-1][side]

    far(0)
    gather_rows(came[0])
    turn_next(near_first)
    arrived.append(cross(crossing[1], arrived[0], near_first))
    crossed_second = cross(other_second, crossed_first, *panels)
    leave = far(1, near_first)
    gather_rows(came[1])
    turn_next(leave, *panels)
    near_crossed_first = swap(after(crossed_first, near_second, arrived[1], came[0][1], from_row(0, 0)), "col", low)
    for j in range(2, chunks):
        if j == 2:
            arrived.append(cross(crossing[j], arrived[1], *panels))
            due = [came[0][1], near_second, from_row(0, 1), from_row(1, 0)]
        else:
            turn_next(near_second, came[0][1], from_row(0, 0), *panels)
            arrived.append(cross(crossing[j], crossed_second, *panels))
            due = [came[1][1], near_crossed_first, from_row(0, 1), from_row(1, 0)]
        far(j, *due)
        gather_rows(came[j])
    near_crossed_second = swap(
        after(crossed_second, near_crossed_first, arrived[-1], came[1][1], from_row(0, 1)), "col", low
    )
    while len(panels) < GROUPS:
        turn_next(from_row(1, 1), *panels)

    def gather_low(found):
        link = Link(1)
        for bit in bits_below(low):
            for e, parts in list(found.items()):
                found[e ^ bit] = [link.swap(p, "col", bit) if bit > 1 else swap(p, "col", bit) for p in parts]
        return [found[e] for e in range(top_col)]

    pieces_mine = gather_low({0: [first, second], low: [near_first, near_second]})
    pieces_crossed = gather_low({0: [crossed_first, crossed_second], low: [near_crossed_first, near_crossed_second]})
    blocks = c_low ^ jnp.arange(top_col, dtype=jnp.int32)
    order = ((blocks // per_block) ^ r_low) * per_block + blocks % per_block

    rb = panel_rows * row_count // mask_panel.shape[0]
    ab = near_l // mask_panel.shape[1]
    row_blocks = panel_rows // rb
    panel_mask = lax.dynamic_slice_in_dim(mask_panel, r * row_blocks, row_blocks, 0)

    near_blocks = near_cols // rb
    near_mask = lax.dynamic_slice_in_dim(mask_near, c * near_blocks, near_blocks, 0)
    near_mask = jnp.repeat(jnp.repeat(near_mask, rb, 0), ab, 1).astype(jnp.bfloat16)
    near = three_near * near_mask[:, None, :]
    green = lax.dynamic_slice_in_dim(green_function, r * share, share, 0)
    dressed = jnp.einsum("qns,ls->nlq", near, green, preferred_element_type=jnp.float32).astype(jnp.bfloat16)

    earlier = (*panels, *[pair[1] for pair in came[2:3]])
    due, begun = [blocks[-1] for blocks in gathered[2:3]], [pair[1] for pair in came[3:4]]
    screened_chunks, contracted_chunks = [], []
    energy = jnp.zeros((tile, tile), jnp.float32)
    hops = {bit: Link(2) for bit in bits_below(row_count)}
    pair = min(PAIR, chunks)
    wide = pair * width
    orders = [bits_below(row_count)[::-1], bits_below(row_count)]
    kept = [[e for e in range(row_count) if not e & bits[0]] for bits in orders]
    places = r ^ jnp.array(kept, jnp.int32)
    first_bits = jnp.array([[bits[0]] for bits in orders], jnp.int32)
    for j in range(0, chunks, pair):
        sources = [[gathered[j + i][f][side] for side in range(2) for i in range(pair)] for f in range(top_row)]
        away = product(pieces_crossed, sources, after(order, *earlier), per_block, jnp.bfloat16)
        home = product(pieces_mine, sources, after(order, away, *begun), per_block, jnp.float32)
        home = home + swap(away, "row", top_row).astype(jnp.float32)
        came_back = swap(home[:, wide:].astype(jnp.bfloat16), "col", top_col)
        screened = (home[:, :wide] + came_back.astype(jnp.float32)).astype(jnp.bfloat16)
        screened_chunks.append(screened)

        gone = contract(panels, screened, panel_mask, after(places ^ first_bits, due), rb, ab, share)
        stay = contract(panels, screened, panel_mask, after(places, gone), rb, ab, share)
        earlier, due, begun = (home, *gone[0], *gone[1]), [], []
        left = [[dict(zip(kept[h], part[h])) for part in (gone, stay)] for h in range(2)]
        for hop in range(len(orders[0])):
            for h, bits in enumerate(orders):
                going, staying = left[h]
                next_bit = bits[hop + 1] if hop + 1 < len(bits) else 0
                total = {}
                for e in sorted(going, key=lambda e: -(e & next_bit)):
                    value = hops[bits[hop]].swap(going[e], "row", bits[hop])
                    begun += [value] if not hop and e & next_bit else []
                    total[e] = (staying[e].astype(jnp.float32) + value.astype(jnp.float32)).astype(jnp.bfloat16)
                left[h] = [
                    {e & ~next_bit: value for e, value in total.items() if e & next_bit},
                    {e: value for e, value in total.items() if not e & next_bit},
                ]
        halves = [left[h][1][0] for h in range(2)]
        contracted_chunks.append(jnp.concatenate(halves))
        parts = [
            jnp.einsum("mlq,nlq->mn", half, dressed[:, :, j * width : j * width + wide], preferred_element_type=jnp.float32)
            for half in halves
        ]
        energy = energy - jnp.concatenate(parts)

    energy = scatter_sum(scatter_sum(energy, "row").T, "col").T
    contracted = jnp.transpose(jnp.concatenate(contracted_chunks, axis=2), (2, 0, 1))
    return jnp.concatenate(screened_chunks, axis=1), contracted, energy


def solution(mesh):
    placed = (
        P("row", "col"),
        P("row", "col"),
        P("row", None, None),
        P("col", None, None),
        P(),
        P(),
        P(),
    )
    return jax.shard_map(
        per_device,
        mesh=mesh,
        in_specs=placed,
        out_specs=(P("row", "col"), P("col", None, "row"), P("row", "col")),
        check_vma=False,
    )
```

```python
import functools

import jax
import jax.numpy as jnp
from jax import lax
from jax.experimental import pallas as pl
from jax.experimental.pallas import tpu as pltpu
from jax.sharding import PartitionSpec as P

WIDTH = 128
PAIR = 2
GROUPS = 4
VMEM = 56
NO_COST = pl.CostEstimate(flops=0, bytes_accessed=0, transcendentals=0)
MIB = 1024 * 1024


def swap(value, axis, bit):
    size = lax.axis_size(axis)
    return lax.ppermute(value, axis, [(i, i ^ bit) for i in range(size)])


def after(value, *others):
    return lax.optimization_barrier((value, others))[0]


class Link:
    def __init__(self, in_flight):
        self.past, self.in_flight = [], in_flight

    def swap(self, value, axis, bit):
        if len(self.past) >= self.in_flight:
            value = after(value, self.past[-self.in_flight])
        self.past.append(swap(value, axis, bit))
        return self.past[-1]


def bits_below(size):
    found = []
    while size > 1:
        size //= 2
        found.append(size)
    return found


def product_kernel(count, parts, per_block, order_ref, *refs):
    pieces, sources, out_ref = refs[: count * parts], refs[count * parts : -6], refs[-6]
    held, weights, total, piece_sems, weight_sems = refs[-5:]
    width = sources[0].shape[2]
    sides = weights.shape[2] // width
    blocks = range(len(sources) // sides)

    def load(e, side, block):
        return pltpu.make_async_copy(
            sources[sides * block + side].at[order_ref[e] % per_block],
            weights.at[e, :, pl.ds(side * width, width)],
            weight_sems.at[e, side],
        )

    rows = pieces[0].shape[0]
    copies = [
        pltpu.make_async_copy(piece, held.at[i // parts, pl.ds(i % parts * rows, rows)], piece_sems.at[i])
        for i, piece in enumerate(pieces)
    ]
    for e in range(count):
        for side in range(sides):
            for block in blocks:

                @pl.when(order_ref[e] // per_block == block)
                def _():
                    load(e, side, block).start()

        for copy in copies[e * parts : (e + 1) * parts]:
            copy.start()
    for e in range(count):
        for side in range(sides):
            load(e, side, 0).wait()
        for copy in copies[e * parts : (e + 1) * parts]:
            copy.wait()
        part = jnp.dot(held[e], weights[e], preferred_element_type=jnp.float32)
        if e == 0:
            total[...] = part
        elif e < count - 1:
            total[...] += part
        else:
            out_ref[...] = (total[...] + part).astype(out_ref.dtype)


def product(pieces, sources, order, per_block, dtype):
    count, parts = len(pieces), len(pieces[0])
    rows, depth = pieces[0][0].shape
    rows *= parts
    sides = len(sources[0])
    cols = sides * sources[0][0].shape[2]
    sources = [part for block in sources for part in block]
    in_hbm = pl.BlockSpec(memory_space=pl.ANY)
    return pl.pallas_call(
        functools.partial(product_kernel, count, parts, per_block),
        in_specs=[pl.BlockSpec(memory_space=pltpu.SMEM)] + [in_hbm] * (count * parts + len(sources)),
        out_specs=pl.BlockSpec(memory_space=pltpu.VMEM),
        out_shape=jax.ShapeDtypeStruct((rows, cols), dtype),
        scratch_shapes=[
            pltpu.VMEM((count, rows, depth), jnp.bfloat16),
            pltpu.VMEM((count, depth, cols), jnp.bfloat16),
            pltpu.VMEM((rows, cols), jnp.float32),
            pltpu.SemaphoreType.DMA((count * parts,)),
            pltpu.SemaphoreType.DMA((count, sides)),
        ],
        compiler_params=pltpu.CompilerParams(vmem_limit_bytes=VMEM * MIB),
        cost_estimate=NO_COST,
    )(order, *[part for piece in pieces for part in piece], *sources)


def turn_kernel(panel_ref, out_ref):
    out_ref[...] = jnp.transpose(panel_ref[...], (1, 2, 0))


def turn(panel, first, rows):
    _, tile, near_l = panel.shape
    tall = tile // GROUPS
    wide = min(rows, 128)
    return pl.pallas_call(
        turn_kernel,
        grid=(rows // wide, tile // tall),
        in_specs=[pl.BlockSpec((wide, tall, near_l), lambda i, g: (first // wide + i, g, 0))],
        out_specs=pl.BlockSpec((tall, near_l, wide), lambda i, g: (g, 0, i)),
        out_shape=jax.ShapeDtypeStruct((tile, near_l, rows), panel.dtype),
        compiler_params=pltpu.CompilerParams(vmem_limit_bytes=VMEM * MIB),
        cost_estimate=NO_COST,
    )(panel)


def contract_kernel(rb, ab, places_ref, mask_ref, screened_ref, *refs):
    count = places_ref.shape[1]
    held, masked, sems = refs[-3:]
    panels, outs = refs[: -3 - 2 * count], refs[-3 - 2 * count : -3]
    _, tall, share, rows = held.shape
    per_share = masked.shape[1]
    each = rows // len(panels)
    half = outs[0].shape[0]
    steps = [(h, i, g) for h in range(2) for i in range(count) for g in range(half // tall)]

    def load(k):
        h, i, g = steps[k]
        at = pl.ds(pl.multiple_of(places_ref[h, i] * share, share), share)
        return [
            pltpu.make_async_copy(
                panel.at[pl.ds(h * half + g * tall, tall), at, :],
                held.at[k % 2, :, :, pl.ds(n * each, each)],
                sems.at[k % 2, n],
            )
            for n, panel in enumerate(panels)
        ]

    for copy in load(0):
        copy.start()
    for k, (h, i, g) in enumerate(steps):
        if k + 1 < len(steps):
            for copy in load(k + 1):
                copy.start()
        if g == 0:
            for b in range(per_share):
                for n in range(rows // rb):
                    part = screened_ref[pl.ds(n * rb, rb), :]
                    flag = mask_ref[n, places_ref[h, i] * per_share + b]
                    masked[i % 2, b, pl.ds(n * rb, rb), :] = jnp.where(flag != 0, part, jnp.zeros_like(part))
        for copy in load(k):
            copy.wait()
        for b in range(per_share):
            block = held[k % 2, :, pl.ds(b * ab, ab), :].reshape(tall * ab, rows)
            part = jnp.dot(block, masked[i % 2, b], preferred_element_type=jnp.float32)
            outs[h * count + i][pl.ds(g * tall, tall), pl.ds(b * ab, ab), :] = part.astype(outs[0].dtype).reshape(
                tall, ab, part.shape[1]
            )


def contract(panels, screened, mask, places, rb, ab, share):
    count = places.shape[1]
    tile, rows = panels[0].shape[0], screened.shape[0]
    tall = tile // GROUPS
    width = screened.shape[1]
    in_smem, in_hbm = pl.BlockSpec(memory_space=pltpu.SMEM), pl.BlockSpec(memory_space=pl.ANY)
    in_vmem = pl.BlockSpec(memory_space=pltpu.VMEM)
    found = pl.pallas_call(
        functools.partial(contract_kernel, rb, ab),
        in_specs=[in_smem, in_smem, in_vmem] + [in_hbm] * len(panels),
        out_specs=[in_vmem] * (2 * count),
        out_shape=[jax.ShapeDtypeStruct((tile // 2, share, width), jnp.bfloat16)] * (2 * count),
        scratch_shapes=[
            pltpu.VMEM((2, tall, share, rows), jnp.bfloat16),
            pltpu.VMEM((2, share // ab, rows, width), jnp.bfloat16),
            pltpu.SemaphoreType.DMA((2, len(panels))),
        ],
        compiler_params=pltpu.CompilerParams(vmem_limit_bytes=VMEM * MIB),
        cost_estimate=NO_COST,
    )(places, mask, screened, *panels)
    return [list(found[:count]), list(found[count:])]


def scatter_sum(value, axis):
    at = lax.axis_index(axis)
    for bit in bits_below(lax.axis_size(axis)):
        halves = value.reshape(2, value.shape[0] // 2, *value.shape[1:])
        mine = (at // bit) % 2
        value = lax.dynamic_index_in_dim(halves, mine, 0, keepdims=False) + swap(
            lax.dynamic_index_in_dim(halves, 1 - mine, 0, keepdims=False), axis, bit
        )
    return value


def per_device(
    polarization, metric, three_panel, three_near, green_function, mask_panel, mask_near
):
    r, c = lax.axis_index("row"), lax.axis_index("col")
    row_count, col_count = lax.axis_size("row"), lax.axis_size("col")
    top_row, top_col = row_count // 2, col_count // 2
    u, v = r // top_row, c // top_col
    r_low, c_low = r % top_row, c % top_col
    panel_rows, depth = polarization.shape
    near_cols = metric.shape[1]
    half = depth // 2
    per_block = metric.shape[0] // depth
    tile, near_l = three_panel.shape[1], three_panel.shape[2]
    share = near_l // row_count
    width = min(WIDTH, near_cols)
    chunks = near_cols // width
    on_diagonal = u == v

    mine = lax.dynamic_slice_in_dim(polarization, u * half, half, 1)
    other = lax.dynamic_slice_in_dim(polarization, (1 - u) * half, half, 1)
    first, second = jnp.split(mine, 2)
    other_first, other_second = jnp.split(other, 2)
    metric_parts = metric.reshape(per_block, 2, half, near_cols)
    metric_mine = lax.dynamic_index_in_dim(metric_parts, u, 1, keepdims=False)
    metric_other = lax.dynamic_index_in_dim(metric_parts, 1 - u, 1, keepdims=False)
    crossing = [metric_other[:, :, j * width : (j + 1) * width] for j in range(chunks)]

    low = top_col // 2

    def cross(value, *others):
        return swap(after(value, *others), "row", top_row)

    arrived, came = [cross(crossing[0])], []
    near_first = swap(first, "col", low)
    crossed_first = cross(other_first, arrived[0])
    near_second = swap(after(second, near_first, arrived[0]), "col", low)
    panels = []

    def turn_next(*others):
        rows = panel_rows // GROUPS
        panels.append(turn(after(three_panel, *others), len(panels) * rows, rows))
        return panels[-1]

    def far(j, *others):
        kept = after(metric_mine, arrived[j])[:, :, j * width : (j + 1) * width]
        stay = jnp.where(on_diagonal, kept, arrived[j])
        leave = jnp.where(on_diagonal, arrived[j], kept)
        came.append([stay, swap(after(leave, *others), "col", top_col)])
        return leave

    row_links = {bit: Link(2) for bit in bits_below(top_row)}

    def gather_rows(pair):
        found = {0: pair}
        for bit in bits_below(top_row):
            for f, parts in list(found.items()):
                found[f ^ bit] = [row_links[bit].swap(p, "row", bit) for p in parts]
        return [found[f] for f in range(top_row)]

    row_links = {bit: Link(2) for bit in bits_below(top_row)}
    gathered = []

    def gather_rows(pair):
        found = {0: pair}
        for bit in bits_below(top_row):
            for f, parts in list(found.items()):
                found[f ^ bit] = [row_links[bit].swap(p, "row", bit) for p in parts]
        gathered.append([found[f] for f in range(top_row)])

    def from_row(j, side):
        return gathered[j][-1][side]

    far(0)
    gather_rows(came[0])
    turn_next(near_first)
    arrived.append(cross(crossing[1], arrived[0], near_first))
    crossed_second = cross(other_second, crossed_first, *panels)
    leave = far(1, near_first)
    gather_rows(came[1])
    turn_next(leave, *panels)
    near_crossed_first = swap(after(crossed_first, near_second, arrived[1], came[0][1], from_row(0, 0)), "col", low)
    for j in range(2, chunks):
        if j == 2:
            arrived.append(cross(crossing[j], arrived[1], *panels))
            due = [came[0][1], near_second, from_row(0, 1), from_row(1, 0)]
        else:
            turn_next(near_second, came[0][1], from_row(0, 0), *panels)
            arrived.append(cross(crossing[j], crossed_second, *panels))
            due = [came[1][1], near_crossed_first, from_row(0, 1), from_row(1, 0)]
        far(j, *due)
        gather_rows(came[j])
    near_crossed_second = swap(
        after(crossed_second, near_crossed_first, arrived[-1], came[1][1], from_row(0, 1)), "col", low
    )
    near_crossed_second = after(near_crossed_second, *[pair[1] for pair in came[2:3]])
    while len(panels) < GROUPS:
        turn_next(from_row(1, 1), *panels)

    def gather_low(found):
        link = Link(1)
        for bit in bits_below(low):
            for e, parts in list(found.items()):
                found[e ^ bit] = [link.swap(p, "col", bit) if bit > 1 else swap(p, "col", bit) for p in parts]
        return [found[e] for e in range(top_col)]

    pieces_mine = gather_low({0: [first, second], low: [near_first, near_second]})
    pieces_crossed = gather_low({0: [crossed_first, crossed_second], low: [near_crossed_first, near_crossed_second]})
    blocks = c_low ^ jnp.arange(top_col, dtype=jnp.int32)
    order = ((blocks // per_block) ^ r_low) * per_block + blocks % per_block

    rb = panel_rows * row_count // mask_panel.shape[0]
    ab = near_l // mask_panel.shape[1]
    row_blocks = panel_rows // rb
    panel_mask = lax.dynamic_slice_in_dim(mask_panel, r * row_blocks, row_blocks, 0)

    earlier = (*panels, *[pair[1] for pair in came[2:3]])
    due, begun = [blocks[-1] for blocks in gathered[2:3]], [pair[1] for pair in came[3:4]]
    screened_chunks, contracted_chunks = [], []
    energy = jnp.zeros((tile, tile), jnp.float32)
    hops = {bit: Link(2) for bit in bits_below(row_count)}
    pair = min(PAIR, chunks)
    wide = pair * width
    orders = [bits_below(row_count)[::-1], bits_below(row_count)]
    kept = [[e for e in range(row_count) if not e & bits[0]] for bits in orders]
    places = r ^ jnp.array(kept, jnp.int32)
    first_bits = jnp.array([[bits[0]] for bits in orders], jnp.int32)
    for j in range(0, chunks, pair):
        sources = [[gathered[j + i][f][side] for side in range(2) for i in range(pair)] for f in range(top_row)]
        away = product(pieces_crossed, sources, after(order, *earlier), per_block, jnp.bfloat16)
        home = product(pieces_mine, sources, after(order, away, *begun), per_block, jnp.float32)
        home = home + swap(away, "row", top_row).astype(jnp.float32)
        came_back = swap(home[:, wide:].astype(jnp.bfloat16), "col", top_col)
        screened = (home[:, :wide] + came_back.astype(jnp.float32)).astype(jnp.bfloat16)
        screened_chunks.append(screened)

        gone = contract(panels, screened, panel_mask, after(places ^ first_bits, due), rb, ab, share)
        stay = contract(panels, screened, panel_mask, after(places, gone), rb, ab, share)
        earlier, due, begun = (home, *gone[0], *gone[1]), [], []
        left = [[dict(zip(kept[h], part[h])) for part in (gone, stay)] for h in range(2)]
        for hop in range(len(orders[0])):
            for h, bits in enumerate(orders):
                going, staying = left[h]
                next_bit = bits[hop + 1] if hop + 1 < len(bits) else 0
                total = {}
                for e in sorted(going, key=lambda e: -(e & next_bit)):
                    value = hops[bits[hop]].swap(going[e], "row", bits[hop])
                    begun += [value] if not hop and e & next_bit else []
                    total[e] = (staying[e].astype(jnp.float32) + value.astype(jnp.float32)).astype(jnp.bfloat16)
                left[h] = [
                    {e & ~next_bit: value for e, value in total.items() if e & next_bit},
                    {e: value for e, value in total.items() if not e & next_bit},
                ]
        halves = [left[h][1][0] for h in range(2)]
        contracted_chunks.append(halves)

    near_blocks = near_cols // rb
    near_mask = lax.dynamic_slice_in_dim(mask_near, c * near_blocks, near_blocks, 0)
    near_mask = jnp.repeat(jnp.repeat(near_mask, rb, 0), ab, 1).astype(jnp.bfloat16)
    near = after(three_near, *stay[0], *stay[1]) * near_mask[:, None, :]
    green = lax.dynamic_slice_in_dim(green_function, r * share, share, 0)
    dressed = jnp.einsum("qns,ls->nlq", near, green, preferred_element_type=jnp.float32).astype(jnp.bfloat16)
    for j, halves in enumerate(contracted_chunks):
        beside = dressed[:, :, j * wide : (j + 1) * wide]
        energy = energy - jnp.concatenate(
            [jnp.einsum("mlq,nlq->mn", half, beside, preferred_element_type=jnp.float32) for half in halves]
        )
    energy = scatter_sum(scatter_sum(energy, "row").T, "col").T
    contracted = jnp.transpose(jnp.concatenate([jnp.concatenate(halves) for halves in contracted_chunks], axis=2), (2, 0, 1))
    return jnp.concatenate(screened_chunks, axis=1), contracted, energy


def solution(mesh):
    placed = (
        P("row", "col"),
        P("row", "col"),
        P("row", None, None),
        P("col", None, None),
        P(),
        P(),
        P(),
    )
    return jax.shard_map(
        per_device,
        mesh=mesh,
        in_specs=placed,
        out_specs=(P("row", "col"), P("col", None, "row"), P("row", "col")),
        check_vma=False,
    )
```

```python
import functools

import jax
import jax.numpy as jnp
from jax import lax
from jax.experimental import pallas as pl
from jax.experimental.pallas import tpu as pltpu
from jax.sharding import PartitionSpec as P

WIDTH = 128
PAIR = 2
GROUPS = 4
VMEM = 56
NO_COST = pl.CostEstimate(flops=0, bytes_accessed=0, transcendentals=0)
MIB = 1024 * 1024


def swap(value, axis, bit):
    size = lax.axis_size(axis)
    return lax.ppermute(value, axis, [(i, i ^ bit) for i in range(size)])


def after(value, *others):
    return lax.optimization_barrier((value, others))[0]


class Link:
    def __init__(self, in_flight):
        self.past, self.in_flight = [], in_flight

    def swap(self, value, axis, bit):
        if len(self.past) >= self.in_flight:
            value = after(value, self.past[-self.in_flight])
        self.past.append(swap(value, axis, bit))
        return self.past[-1]


def bits_below(size):
    found = []
    while size > 1:
        size //= 2
        found.append(size)
    return found


def product_kernel(count, parts, per_block, order_ref, *refs):
    pieces, sources, out_ref = refs[: count * parts], refs[count * parts : -6], refs[-6]
    held, weights, total, piece_sems, weight_sems = refs[-5:]
    width = sources[0].shape[2]
    sides = weights.shape[2] // width
    blocks = range(len(sources) // sides)

    def load(e, side, block):
        return pltpu.make_async_copy(
            sources[sides * block + side].at[order_ref[e] % per_block],
            weights.at[e, :, pl.ds(side * width, width)],
            weight_sems.at[e, side],
        )

    rows = pieces[0].shape[0]
    copies = [
        pltpu.make_async_copy(piece, held.at[i // parts, pl.ds(i % parts * rows, rows)], piece_sems.at[i])
        for i, piece in enumerate(pieces)
    ]
    for e in range(count):
        for side in range(sides):
            for block in blocks:

                @pl.when(order_ref[e] // per_block == block)
                def _():
                    load(e, side, block).start()

        for copy in copies[e * parts : (e + 1) * parts]:
            copy.start()
    for e in range(count):
        for side in range(sides):
            load(e, side, 0).wait()
        for copy in copies[e * parts : (e + 1) * parts]:
            copy.wait()
        part = jnp.dot(held[e], weights[e], preferred_element_type=jnp.float32)
        if e == 0:
            total[...] = part
        elif e < count - 1:
            total[...] += part
        else:
            out_ref[...] = (total[...] + part).astype(out_ref.dtype)


def product(pieces, sources, order, per_block, dtype):
    count, parts = len(pieces), len(pieces[0])
    rows, depth = pieces[0][0].shape
    rows *= parts
    sides = len(sources[0])
    cols = sides * sources[0][0].shape[2]
    sources = [part for block in sources for part in block]
    in_hbm = pl.BlockSpec(memory_space=pl.ANY)
    return pl.pallas_call(
        functools.partial(product_kernel, count, parts, per_block),
        in_specs=[pl.BlockSpec(memory_space=pltpu.SMEM)] + [in_hbm] * (count * parts + len(sources)),
        out_specs=pl.BlockSpec(memory_space=pltpu.VMEM),
        out_shape=jax.ShapeDtypeStruct((rows, cols), dtype),
        scratch_shapes=[
            pltpu.VMEM((count, rows, depth), jnp.bfloat16),
            pltpu.VMEM((count, depth, cols), jnp.bfloat16),
            pltpu.VMEM((rows, cols), jnp.float32),
            pltpu.SemaphoreType.DMA((count * parts,)),
            pltpu.SemaphoreType.DMA((count, sides)),
        ],
        compiler_params=pltpu.CompilerParams(vmem_limit_bytes=VMEM * MIB),
        cost_estimate=NO_COST,
    )(order, *[part for piece in pieces for part in piece], *sources)


def turn_kernel(panel_ref, out_ref):
    out_ref[...] = jnp.transpose(panel_ref[...], (1, 2, 0))


def turn(panel, first, rows):
    _, tile, near_l = panel.shape
    tall = tile // GROUPS
    wide = min(rows, 128)
    return pl.pallas_call(
        turn_kernel,
        grid=(rows // wide, tile // tall),
        in_specs=[pl.BlockSpec((wide, tall, near_l), lambda i, g: (first // wide + i, g, 0))],
        out_specs=pl.BlockSpec((tall, near_l, wide), lambda i, g: (g, 0, i)),
        out_shape=jax.ShapeDtypeStruct((tile, near_l, rows), panel.dtype),
        compiler_params=pltpu.CompilerParams(vmem_limit_bytes=VMEM * MIB),
        cost_estimate=pl.CostEstimate(flops=0, bytes_accessed=8 * rows * tile * near_l, transcendentals=0),
    )(panel)


def contract_kernel(rb, ab, places_ref, mask_ref, screened_ref, *refs):
    count = places_ref.shape[1]
    held, masked, sems = refs[-3:]
    panels, outs = refs[: -3 - 2 * count], refs[-3 - 2 * count : -3]
    _, tall, share, rows = held.shape
    per_share = masked.shape[1]
    each = rows // len(panels)
    half = outs[0].shape[0]
    steps = [(h, i, g) for h in range(2) for i in range(count) for g in range(half // tall)]

    def load(k):
        h, i, g = steps[k]
        at = pl.ds(pl.multiple_of(places_ref[h, i] * share, share), share)
        return [
            pltpu.make_async_copy(
                panel.at[pl.ds(h * half + g * tall, tall), at, :],
                held.at[k % 2, :, :, pl.ds(n * each, each)],
                sems.at[k % 2, n],
            )
            for n, panel in enumerate(panels)
        ]

    for copy in load(0):
        copy.start()
    for k, (h, i, g) in enumerate(steps):
        if k + 1 < len(steps):
            for copy in load(k + 1):
                copy.start()
        if g == 0:
            for b in range(per_share):
                for n in range(rows // rb):
                    part = screened_ref[pl.ds(n * rb, rb), :]
                    flag = mask_ref[n, places_ref[h, i] * per_share + b]
                    masked[i % 2, b, pl.ds(n * rb, rb), :] = jnp.where(flag != 0, part, jnp.zeros_like(part))
        for copy in load(k):
            copy.wait()
        for b in range(per_share):
            block = held[k % 2, :, pl.ds(b * ab, ab), :].reshape(tall * ab, rows)
            part = jnp.dot(block, masked[i % 2, b], preferred_element_type=jnp.float32)
            outs[h * count + i][pl.ds(g * tall, tall), pl.ds(b * ab, ab), :] = part.astype(outs[0].dtype).reshape(
                tall, ab, part.shape[1]
            )


def contract(panels, screened, mask, places, rb, ab, share):
    count = places.shape[1]
    tile, rows = panels[0].shape[0], screened.shape[0]
    tall = tile // GROUPS
    width = screened.shape[1]
    in_smem, in_hbm = pl.BlockSpec(memory_space=pltpu.SMEM), pl.BlockSpec(memory_space=pl.ANY)
    in_vmem = pl.BlockSpec(memory_space=pltpu.VMEM)
    found = pl.pallas_call(
        functools.partial(contract_kernel, rb, ab),
        in_specs=[in_smem, in_smem, in_vmem] + [in_hbm] * len(panels),
        out_specs=[in_vmem] * (2 * count),
        out_shape=[jax.ShapeDtypeStruct((tile // 2, share, width), jnp.bfloat16)] * (2 * count),
        scratch_shapes=[
            pltpu.VMEM((2, tall, share, rows), jnp.bfloat16),
            pltpu.VMEM((2, share // ab, rows, width), jnp.bfloat16),
            pltpu.SemaphoreType.DMA((2, len(panels))),
        ],
        compiler_params=pltpu.CompilerParams(vmem_limit_bytes=VMEM * MIB),
        cost_estimate=NO_COST,
    )(places, mask, screened, *panels)
    return [list(found[:count]), list(found[count:])]


def scatter_sum(value, axis):
    at = lax.axis_index(axis)
    for bit in bits_below(lax.axis_size(axis)):
        halves = value.reshape(2, value.shape[0] // 2, *value.shape[1:])
        mine = (at // bit) % 2
        value = lax.dynamic_index_in_dim(halves, mine, 0, keepdims=False) + swap(
            lax.dynamic_index_in_dim(halves, 1 - mine, 0, keepdims=False), axis, bit
        )
    return value


def per_device(
    polarization, metric, three_panel, three_near, green_function, mask_panel, mask_near
):
    r, c = lax.axis_index("row"), lax.axis_index("col")
    row_count, col_count = lax.axis_size("row"), lax.axis_size("col")
    top_row, top_col = row_count // 2, col_count // 2
    u, v = r // top_row, c // top_col
    r_low, c_low = r % top_row, c % top_col
    panel_rows, depth = polarization.shape
    near_cols = metric.shape[1]
    half = depth // 2
    per_block = metric.shape[0] // depth
    tile, near_l = three_panel.shape[1], three_panel.shape[2]
    share = near_l // row_count
    width = min(WIDTH, near_cols)
    chunks = near_cols // width
    on_diagonal = u == v

    mine = lax.dynamic_slice_in_dim(polarization, u * half, half, 1)
    other = lax.dynamic_slice_in_dim(polarization, (1 - u) * half, half, 1)
    first, second = jnp.split(mine, 2)
    other_first, other_second = jnp.split(other, 2)
    metric_parts = metric.reshape(per_block, 2, half, near_cols)
    metric_mine = lax.dynamic_index_in_dim(metric_parts, u, 1, keepdims=False)
    metric_other = lax.dynamic_index_in_dim(metric_parts, 1 - u, 1, keepdims=False)
    crossing = [metric_other[:, :, j * width : (j + 1) * width] for j in range(chunks)]

    rb = panel_rows * row_count // mask_panel.shape[0]
    ab = near_l // mask_panel.shape[1]
    row_blocks = panel_rows // rb
    panel_mask = lax.dynamic_slice_in_dim(mask_panel, r * row_blocks, row_blocks, 0)

    low = top_col // 2

    def cross(value, *others):
        return swap(after(value, *others), "row", top_row)

    arrived, came = [cross(crossing[0])], []
    near_first = swap(first, "col", low)
    crossed_first = cross(other_first, arrived[0])
    near_second = swap(after(second, near_first, arrived[0]), "col", low)
    panels = []

    def turn_next(*others):
        rows = panel_rows // GROUPS
        panels.append(turn(after(three_panel, *others), len(panels) * rows, rows))
        return panels[-1]

    def far(j, *others):
        kept = after(metric_mine, arrived[j])[:, :, j * width : (j + 1) * width]
        stay = jnp.where(on_diagonal, kept, arrived[j])
        leave = jnp.where(on_diagonal, arrived[j], kept)
        came.append([stay, swap(after(leave, *others), "col", top_col)])
        return leave

    row_links = {bit: Link(2) for bit in bits_below(top_row)}

    def gather_rows(pair):
        found = {0: pair}
        for bit in bits_below(top_row):
            for f, parts in list(found.items()):
                found[f ^ bit] = [row_links[bit].swap(p, "row", bit) for p in parts]
        return [found[f] for f in range(top_row)]

    row_links = {bit: Link(2) for bit in bits_below(top_row)}
    gathered = []

    def gather_rows(pair):
        found = {0: pair}
        for bit in bits_below(top_row):
            for f, parts in list(found.items()):
                found[f ^ bit] = [row_links[bit].swap(p, "row", bit) for p in parts]
        gathered.append([found[f] for f in range(top_row)])

    def from_row(j, side):
        return gathered[j][-1][side]

    far(0)
    gather_rows(came[0])
    turn_next(near_first)
    arrived.append(cross(crossing[1], arrived[0], near_first))
    crossed_second = cross(other_second, crossed_first, *panels)
    leave = far(1, near_first)
    gather_rows(came[1])
    turn_next(leave, *panels)
    near_crossed_first = swap(after(crossed_first, near_second, arrived[1], came[0][1], from_row(0, 0)), "col", low)
    for j in range(2, chunks):
        due = [came[j - 2][1], near_second, from_row(0, 1), from_row(1, 0)]
        if j == 2:
            arrived.append(cross(crossing[j], arrived[1], *panels))
        else:
            due.append(near_crossed_first)
            while len(panels) < GROUPS:
                turn_next(near_second, came[0][1], from_row(0, 0), *panels)
            arrived.append(cross(crossing[j], crossed_second, *panels))
        far(j, *due)
    while len(panels) < GROUPS:
        turn_next(near_second, *panels)

    near_blocks = near_cols // rb
    near_mask = lax.dynamic_slice_in_dim(mask_near, c * near_blocks, near_blocks, 0)
    near_mask = jnp.repeat(jnp.repeat(near_mask, rb, 0), ab, 1).astype(jnp.bfloat16)
    near = after(three_near, near_crossed_first, came[1][1]) * near_mask[:, None, :]
    green = lax.dynamic_slice_in_dim(green_function, r * share, share, 0)
    dressed = jnp.einsum("qns,ls->nlq", near, green, preferred_element_type=jnp.float32).astype(jnp.bfloat16)

    near_crossed_second = swap(
        after(crossed_second, near_crossed_first, arrived[-1], came[1][1], from_row(0, 1)), "col", low
    )
    near_crossed_second = after(near_crossed_second, dressed, *panels, *[pair[1] for pair in came[2:3]])

    def gather_low(found):
        link = Link(1)
        for bit in bits_below(low):
            for e, parts in list(found.items()):
                found[e ^ bit] = [link.swap(p, "col", bit) if bit > 1 else swap(p, "col", bit) for p in parts]
        return [found[e] for e in range(top_col)]

    pieces_mine = gather_low({0: [first, second], low: [near_first, near_second]})
    pieces_crossed = gather_low({0: [crossed_first, crossed_second], low: [near_crossed_first, near_crossed_second]})
    blocks = c_low ^ jnp.arange(top_col, dtype=jnp.int32)
    order = ((blocks // per_block) ^ r_low) * per_block + blocks % per_block

    earlier, due = (), [pair[1] for pair in came[3:4]]
    ready = pieces_crossed[-1][-1]
    screened_chunks, contracted_chunks = [], []
    energy = jnp.zeros((tile, tile), jnp.float32)
    hops = {bit: Link(2) for bit in bits_below(row_count)}
    pair = min(PAIR, chunks)
    wide = pair * width
    orders = [bits_below(row_count)[::-1], bits_below(row_count)]
    kept = [[e for e in range(row_count) if not e & bits[0]] for bits in orders]
    places = r ^ jnp.array(kept, jnp.int32)
    first_bits = jnp.array([[bits[0]] for bits in orders], jnp.int32)
    for j in range(0, chunks, pair):
        for i in range(len(gathered), min(j + pair + 1, chunks)):
            gather_rows([after(part, ready) for part in came[i]])
        sources = [[gathered[j + i][f][side] for side in range(2) for i in range(pair)] for f in range(top_row)]
        away = product(pieces_crossed, sources, after(order, *earlier), per_block, jnp.bfloat16)
        ready = away
        home = product(pieces_mine, sources, after(order, away), per_block, jnp.float32)
        home = after(home, *due) + swap(away, "row", top_row).astype(jnp.float32)
        came_back = swap(home[:, wide:].astype(jnp.bfloat16), "col", top_col)
        screened = (home[:, :wide] + came_back.astype(jnp.float32)).astype(jnp.bfloat16)
        screened_chunks.append(screened)

        gone = contract(panels, screened, panel_mask, places ^ first_bits, rb, ab, share)
        stay = contract(panels, screened, panel_mask, after(places, gone), rb, ab, share)
        earlier, due = (home, *gone[0], *gone[1]), []
        left = [[dict(zip(kept[h], part[h])) for part in (gone, stay)] for h in range(2)]
        for hop in range(len(orders[0])):
            for h, bits in enumerate(orders):
                going, staying = left[h]
                next_bit = bits[hop + 1] if hop + 1 < len(bits) else 0
                total = {}
                for e in sorted(going, key=lambda e: -(e & next_bit)):
                    value = hops[bits[hop]].swap(going[e], "row", bits[hop])
                    due += [value] if not hop and e & next_bit else []
                    total[e] = (staying[e].astype(jnp.float32) + value.astype(jnp.float32)).astype(jnp.bfloat16)
                left[h] = [
                    {e & ~next_bit: value for e, value in total.items() if e & next_bit},
                    {e: value for e, value in total.items() if not e & next_bit},
                ]
        halves = [left[h][1][0] for h in range(2)]
        contracted_chunks.append(halves)

    for j, halves in enumerate(contracted_chunks):
        beside = dressed[:, :, j * wide : (j + 1) * wide]
        energy = energy - jnp.concatenate(
            [jnp.einsum("mlq,nlq->mn", half, beside, preferred_element_type=jnp.float32) for half in halves]
        )
    contracted = jnp.transpose(jnp.concatenate([jnp.concatenate(halves) for halves in contracted_chunks], axis=2), (2, 0, 1))
    energy = scatter_sum(after(scatter_sum(energy, "row"), contracted).T, "col").T
    return jnp.concatenate(screened_chunks, axis=1), contracted, energy


def solution(mesh):
    placed = (
        P("row", "col"),
        P("row", "col"),
        P("row", None, None),
        P("col", None, None),
        P(),
        P(),
        P(),
    )
    return jax.shard_map(
        per_device,
        mesh=mesh,
        in_specs=placed,
        out_specs=(P("row", "col"), P("col", None, "row"), P("row", "col")),
        check_vma=False,
    )
```

```python
import functools

import jax
import jax.numpy as jnp
from jax import lax
from jax.experimental import pallas as pl
from jax.experimental.pallas import tpu as pltpu
from jax.sharding import PartitionSpec as P

WIDTH = 128
GROUPS = 4
VMEM = 56
MIB = 1024 * 1024
NO_COST = pl.CostEstimate(flops=0, bytes_accessed=0, transcendentals=0)


def swap(value, axis, bit):
    size = lax.axis_size(axis)
    return lax.ppermute(value, axis, [(i, i ^ bit) for i in range(size)])


def after(value, *others):
    return lax.optimization_barrier((value, others))[0]


class Link:
    def __init__(self, in_flight):
        self.past, self.in_flight = [], in_flight

    def swap(self, value, axis, bit):
        if len(self.past) >= self.in_flight:
            value = after(value, self.past[-self.in_flight])
        self.past.append(swap(value, axis, bit))
        return self.past[-1]


def bits_below(size):
    found = []
    while size > 1:
        size //= 2
        found.append(size)
    return found


def product_kernel(count, parts, per_block, order_ref, *refs):
    pieces, sources, out_ref = refs[: count * parts], refs[count * parts : -6], refs[-6]
    held, weights, total, piece_sems, weight_sems = refs[-5:]
    width = sources[0].shape[2]
    sides = weights.shape[2] // width
    blocks = range(len(sources) // sides)

    def load(e, side, block):
        return pltpu.make_async_copy(
            sources[sides * block + side].at[order_ref[e] % per_block],
            weights.at[e, :, pl.ds(side * width, width)],
            weight_sems.at[e, side],
        )

    rows = pieces[0].shape[0]
    copies = [
        pltpu.make_async_copy(piece, held.at[i // parts, pl.ds(i % parts * rows, rows)], piece_sems.at[i])
        for i, piece in enumerate(pieces)
    ]
    for e in range(count):
        for side in range(sides):
            for block in blocks:

                @pl.when(order_ref[e] // per_block == block)
                def _():
                    load(e, side, block).start()

        for copy in copies[e * parts : (e + 1) * parts]:
            copy.start()
    for e in range(count):
        for side in range(sides):
            load(e, side, 0).wait()
        for copy in copies[e * parts : (e + 1) * parts]:
            copy.wait()
        part = jnp.dot(held[e], weights[e], preferred_element_type=jnp.float32)
        if e == 0:
            total[...] = part
        elif e < count - 1:
            total[...] += part
        else:
            out_ref[...] = (total[...] + part).astype(out_ref.dtype)


def product(pieces, sources, order, per_block, dtype):
    count, parts = len(pieces), len(pieces[0])
    rows, depth = pieces[0][0].shape
    rows *= parts
    sides = len(sources[0])
    cols = sides * sources[0][0].shape[2]
    sources = [part for block in sources for part in block]
    in_hbm = pl.BlockSpec(memory_space=pl.ANY)
    return pl.pallas_call(
        functools.partial(product_kernel, count, parts, per_block),
        in_specs=[pl.BlockSpec(memory_space=pltpu.SMEM)] + [in_hbm] * (count * parts + len(sources)),
        out_specs=pl.BlockSpec(memory_space=pltpu.VMEM),
        out_shape=jax.ShapeDtypeStruct((rows, cols), dtype),
        scratch_shapes=[
            pltpu.VMEM((count, rows, depth), jnp.bfloat16),
            pltpu.VMEM((count, depth, cols), jnp.bfloat16),
            pltpu.VMEM((rows, cols), jnp.float32),
            pltpu.SemaphoreType.DMA((count * parts,)),
            pltpu.SemaphoreType.DMA((count, sides)),
        ],
        compiler_params=pltpu.CompilerParams(vmem_limit_bytes=VMEM * MIB),
        cost_estimate=NO_COST,
    )(order, *[part for piece in pieces for part in piece], *sources)


def turn_kernel(panel_ref, out_ref):
    out_ref[...] = jnp.transpose(panel_ref[...], (1, 2, 0))


def turn(panel, first, rows):
    _, tile, near_l = panel.shape
    tall = tile // GROUPS
    wide = min(rows, 128)
    return pl.pallas_call(
        turn_kernel,
        grid=(rows // wide, tile // tall),
        in_specs=[pl.BlockSpec((wide, tall, near_l), lambda i, g: (first // wide + i, g, 0))],
        out_specs=pl.BlockSpec((tall, near_l, wide), lambda i, g: (g, 0, i)),
        out_shape=jax.ShapeDtypeStruct((tile, near_l, rows), panel.dtype),
        compiler_params=pltpu.CompilerParams(vmem_limit_bytes=VMEM * MIB),
        cost_estimate=pl.CostEstimate(flops=0, bytes_accessed=8 * rows * tile * near_l, transcendentals=0),
    )(panel)


def contract_kernel(rb, ab, places_ref, mask_ref, screened_ref, *refs):
    count = places_ref.shape[1]
    held, masked, sems = refs[-3:]
    panels, outs = refs[: -3 - 2 * count], refs[-3 - 2 * count : -3]
    _, tall, share, rows = held.shape
    per_share = masked.shape[1]
    each = rows // len(panels)
    half = outs[0].shape[0]
    steps = [(h, i, g) for h in range(2) for i in range(count) for g in range(half // tall)]

    def load(k):
        h, i, g = steps[k]
        at = pl.ds(pl.multiple_of(places_ref[h, i] * share, share), share)
        return [
            pltpu.make_async_copy(
                panel.at[pl.ds(h * half + g * tall, tall), at, :],
                held.at[k % 2, :, :, pl.ds(n * each, each)],
                sems.at[k % 2, n],
            )
            for n, panel in enumerate(panels)
        ]

    for copy in load(0):
        copy.start()
    for k, (h, i, g) in enumerate(steps):
        if k + 1 < len(steps):
            for copy in load(k + 1):
                copy.start()
        if g == 0:
            for b in range(per_share):
                for n in range(rows // rb):
                    part = screened_ref[pl.ds(n * rb, rb), :]
                    flag = mask_ref[n, places_ref[h, i] * per_share + b]
                    masked[i % 2, b, pl.ds(n * rb, rb), :] = jnp.where(flag != 0, part, jnp.zeros_like(part))
        for copy in load(k):
            copy.wait()
        for b in range(per_share):
            block = held[k % 2, :, pl.ds(b * ab, ab), :].reshape(tall * ab, rows)
            part = jnp.dot(block, masked[i % 2, b], preferred_element_type=jnp.float32)
            outs[h * count + i][pl.ds(g * tall, tall), pl.ds(b * ab, ab), :] = part.astype(outs[0].dtype).reshape(
                tall, ab, part.shape[1]
            )


def contract(panels, screened, mask, places, rb, ab, share):
    count = places.shape[1]
    tile, rows = panels[0].shape[0], screened.shape[0]
    tall = tile // GROUPS
    width = screened.shape[1]
    in_smem, in_hbm = pl.BlockSpec(memory_space=pltpu.SMEM), pl.BlockSpec(memory_space=pl.ANY)
    in_vmem = pl.BlockSpec(memory_space=pltpu.VMEM)
    found = pl.pallas_call(
        functools.partial(contract_kernel, rb, ab),
        in_specs=[in_smem, in_smem, in_vmem] + [in_hbm] * len(panels),
        out_specs=[in_vmem] * (2 * count),
        out_shape=[jax.ShapeDtypeStruct((tile // 2, share, width), jnp.bfloat16)] * (2 * count),
        scratch_shapes=[
            pltpu.VMEM((2, tall, share, rows), jnp.bfloat16),
            pltpu.VMEM((2, share // ab, rows, width), jnp.bfloat16),
            pltpu.SemaphoreType.DMA((2, len(panels))),
        ],
        compiler_params=pltpu.CompilerParams(vmem_limit_bytes=VMEM * MIB),
        cost_estimate=NO_COST,
    )(places, mask, screened, *panels)
    return [list(found[:count]), list(found[count:])]


def scatter_sum(value, axis):
    at = lax.axis_index(axis)
    for bit in bits_below(lax.axis_size(axis)):
        halves = value.reshape(2, value.shape[0] // 2, *value.shape[1:])
        mine = (at // bit) % 2
        value = lax.dynamic_index_in_dim(halves, mine, 0, keepdims=False) + swap(
            lax.dynamic_index_in_dim(halves, 1 - mine, 0, keepdims=False), axis, bit
        )
    return value


def per_device(
    polarization, metric, three_panel, three_near, green_function, mask_panel, mask_near
):
    r, c = lax.axis_index("row"), lax.axis_index("col")
    row_count, col_count = lax.axis_size("row"), lax.axis_size("col")
    top_row, top_col = row_count // 2, col_count // 2
    u, v = r // top_row, c // top_col
    r_low, c_low = r % top_row, c % top_col
    panel_rows, depth = polarization.shape
    near_cols = metric.shape[1]
    half = depth // 2
    per_block = metric.shape[0] // depth
    tile, near_l = three_panel.shape[1], three_panel.shape[2]
    share = near_l // row_count
    wide = near_cols // 2 if near_cols >= 4 * WIDTH else near_cols
    width = wide // 2
    bounds = [(0, width), (width, width)] + ([(wide, wide)] if wide < near_cols else [])
    chunks = len(bounds)
    on_diagonal = u == v

    mine = lax.dynamic_slice_in_dim(polarization, u * half, half, 1)
    other = lax.dynamic_slice_in_dim(polarization, (1 - u) * half, half, 1)
    first, second = jnp.split(mine, 2)
    other_first, other_second = jnp.split(other, 2)
    metric_parts = metric.reshape(per_block, 2, half, near_cols)
    metric_mine = lax.dynamic_index_in_dim(metric_parts, u, 1, keepdims=False)
    metric_other = lax.dynamic_index_in_dim(metric_parts, 1 - u, 1, keepdims=False)
    crossing = [metric_other[:, :, at : at + size] for at, size in bounds]

    rb = panel_rows * row_count // mask_panel.shape[0]
    ab = near_l // mask_panel.shape[1]
    row_blocks = panel_rows // rb
    panel_mask = lax.dynamic_slice_in_dim(mask_panel, r * row_blocks, row_blocks, 0)

    low = top_col // 2

    def cross(value, *others):
        return swap(after(value, *others), "row", top_row)

    arrived, came = [cross(crossing[0])], []
    near_first = swap(first, "col", low)
    crossed_first = cross(other_first, arrived[0])
    near_second = swap(after(second, near_first, arrived[0]), "col", low)
    panels = []

    def turn_next(*others):
        rows = panel_rows // GROUPS
        panels.append(turn(after(three_panel, *others), len(panels) * rows, rows))
        return panels[-1]

    def far(j, *others):
        at, size = bounds[j]
        kept = after(metric_mine, arrived[j])[:, :, at : at + size]
        stay = jnp.where(on_diagonal, kept, arrived[j])
        leave = jnp.where(on_diagonal, arrived[j], kept)
        came.append([stay, swap(after(leave, *others), "col", top_col)])
        return leave

    row_links = {bit: Link(2) for bit in bits_below(top_row)}

    def gather_rows(pair):
        found = {0: pair}
        for bit in bits_below(top_row):
            for f, parts in list(found.items()):
                found[f ^ bit] = [row_links[bit].swap(p, "row", bit) for p in parts]
        return [found[f] for f in range(top_row)]

    row_links = {bit: Link(2) for bit in bits_below(top_row)}
    gathered = []

    def gather_rows(pair):
        found = {0: pair}
        for bit in bits_below(top_row):
            for f, parts in list(found.items()):
                found[f ^ bit] = [row_links[bit].swap(p, "row", bit) for p in parts]
        gathered.append([found[f] for f in range(top_row)])

    def from_row(j, side):
        return gathered[j][-1][side]

    far(0)
    gather_rows(came[0])
    turn_next(near_first)
    arrived.append(cross(crossing[1], arrived[0], near_first))
    crossed_second = cross(other_second, crossed_first, *panels)
    leave = far(1, near_first)
    gather_rows(came[1])
    turn_next(leave, *panels)
    near_crossed_first = swap(after(crossed_first, near_second, arrived[1], came[0][1], from_row(0, 0)), "col", low)
    for j in range(2, chunks):
        arrived.append(cross(crossing[j], arrived[1], *panels))
        far(j, came[j - 2][1], near_second, from_row(0, 1), from_row(1, 0))
        gather_rows(came[j][:1])
    while len(panels) < GROUPS:
        turn_next(near_second, came[0][1], from_row(0, 0), *panels)

    near_blocks = near_cols // rb
    near_mask = lax.dynamic_slice_in_dim(mask_near, c * near_blocks, near_blocks, 0)
    near_mask = jnp.repeat(jnp.repeat(near_mask, rb, 0), ab, 1).astype(jnp.bfloat16)
    near = after(three_near, near_crossed_first, came[1][1]) * near_mask[:, None, :]
    green = lax.dynamic_slice_in_dim(green_function, r * share, share, 0)
    dressed = jnp.einsum("qns,ls->nlq", near, green, preferred_element_type=jnp.float32).astype(jnp.bfloat16)

    near_crossed_second = swap(
        after(crossed_second, near_crossed_first, arrived[-1], came[1][1], from_row(0, 1)), "col", low
    )
    due = [part for j in range(2, chunks) for part in (came[j][1], from_row(j, 0))]
    near_crossed_second = after(near_crossed_second, dressed, *panels, *due)

    def gather_low(found):
        link = Link(1)
        for bit in bits_below(low):
            for e, parts in list(found.items()):
                found[e ^ bit] = [link.swap(p, "col", bit) if bit > 1 else swap(p, "col", bit) for p in parts]
        return [found[e] for e in range(top_col)]

    pieces_mine = gather_low({0: [first, second], low: [near_first, near_second]})
    pieces_crossed = gather_low({0: [crossed_first, crossed_second], low: [near_crossed_first, near_crossed_second]})
    blocks = c_low ^ jnp.arange(top_col, dtype=jnp.int32)
    order = ((blocks // per_block) ^ r_low) * per_block + blocks % per_block

    screened_chunks, contracted_chunks = [], []
    energy = jnp.zeros((tile, tile), jnp.float32)
    hops = {bit: Link(2) for bit in bits_below(row_count)}
    orders = [bits_below(row_count)[::-1], bits_below(row_count)]
    kept = [[e for e in range(row_count) if not e & bits[0]] for bits in orders]
    places = r ^ jnp.array(kept, jnp.int32)
    first_bits = jnp.array([[bits[0]] for bits in orders], jnp.int32)
    groups = [[0, 1]] + [[j] for j in range(2, chunks)]

    def sources_of(k):
        return [[gathered[i][f][side] for side in range(2) for i in groups[k]] for f in range(top_row)]

    away = product(pieces_crossed, sources_of(0), order, per_block, jnp.bfloat16)
    for j in range(2, chunks):
        early = gathered.pop(2)
        gather_rows([after(came[j][1], pieces_crossed[-1][-1])])
        gathered.append([a + b for a, b in zip(early, gathered.pop())])
    home = product(pieces_mine, sources_of(0), after(order, away), per_block, jnp.float32)
    due = []
    for k in range(len(groups)):
        total = after(home, *due) + swap(away, "row", top_row).astype(jnp.float32)
        came_back = swap(total[:, wide:].astype(jnp.bfloat16), "col", top_col)
        screened = (total[:, :wide] + came_back.astype(jnp.float32)).astype(jnp.bfloat16)
        screened_chunks.append(screened)

        if k + 1 < len(groups):
            away = product(pieces_crossed, sources_of(k + 1), after(order, home), per_block, jnp.bfloat16)
        gone = contract(panels, screened, panel_mask, after(places ^ first_bits, away), rb, ab, share)
        if k + 1 < len(groups):
            home = product(pieces_mine, sources_of(k + 1), after(order, away, gone), per_block, jnp.float32)
        stay = contract(panels, screened, panel_mask, after(places, home, gone), rb, ab, share)
        due = []
        left = [[dict(zip(kept[h], part[h])) for part in (gone, stay)] for h in range(2)]
        for hop in range(len(orders[0])):
            for h, bits in enumerate(orders):
                going, staying = left[h]
                next_bit = bits[hop + 1] if hop + 1 < len(bits) else 0
                total = {}
                for e in sorted(going, key=lambda e: -(e & next_bit)):
                    value = hops[bits[hop]].swap(going[e], "row", bits[hop])
                    due += [value] if not hop and e & next_bit else []
                    total[e] = (staying[e].astype(jnp.float32) + value.astype(jnp.float32)).astype(jnp.bfloat16)
                left[h] = [
                    {e & ~next_bit: value for e, value in total.items() if e & next_bit},
                    {e: value for e, value in total.items() if not e & next_bit},
                ]
        halves = [left[h][1][0] for h in range(2)]
        contracted_chunks.append(halves)

    for j, halves in enumerate(contracted_chunks):
        beside = dressed[:, :, j * wide : (j + 1) * wide]
        energy = energy - jnp.concatenate(
            [jnp.einsum("mlq,nlq->mn", half, beside, preferred_element_type=jnp.float32) for half in halves]
        )
    contracted = jnp.transpose(jnp.concatenate([jnp.concatenate(halves) for halves in contracted_chunks], axis=2), (2, 0, 1))
    energy = scatter_sum(after(scatter_sum(energy, "row"), contracted).T, "col").T
    return jnp.concatenate(screened_chunks, axis=1), contracted, energy


def solution(mesh):
    placed = (
        P("row", "col"),
        P("row", "col"),
        P("row", None, None),
        P("col", None, None),
        P(),
        P(),
        P(),
    )
    return jax.shard_map(
        per_device,
        mesh=mesh,
        in_specs=placed,
        out_specs=(P("row", "col"), P("col", None, "row"), P("row", "col")),
        check_vma=False,
    )
```

```python
import functools

import jax
import jax.numpy as jnp
from jax import lax
from jax.experimental import pallas as pl
from jax.experimental.pallas import tpu as pltpu
from jax.sharding import PartitionSpec as P

WIDTH = 128
PAIR = 2
GROUPS = 4
VMEM = 56
NO_COST = pl.CostEstimate(flops=0, bytes_accessed=0, transcendentals=0)
MIB = 1024 * 1024


def swap(value, axis, bit):
    size = lax.axis_size(axis)
    return lax.ppermute(value, axis, [(i, i ^ bit) for i in range(size)])


def after(value, *others):
    return lax.optimization_barrier((value, others))[0]


class Link:
    def __init__(self, in_flight):
        self.past, self.in_flight = [], in_flight

    def swap(self, value, axis, bit):
        if len(self.past) >= self.in_flight:
            value = after(value, self.past[-self.in_flight])
        self.past.append(swap(value, axis, bit))
        return self.past[-1]


def bits_below(size):
    found = []
    while size > 1:
        size //= 2
        found.append(size)
    return found


def product_kernel(count, parts, per_block, order_ref, *refs):
    pieces, sources, out_ref = refs[: count * parts], refs[count * parts : -6], refs[-6]
    held, weights, total, piece_sems, weight_sems = refs[-5:]
    width = sources[0].shape[2]
    sides = weights.shape[2] // width
    blocks = range(len(sources) // sides)

    def load(e, side, block):
        return pltpu.make_async_copy(
            sources[sides * block + side].at[order_ref[e] % per_block],
            weights.at[e, :, pl.ds(side * width, width)],
            weight_sems.at[e, side],
        )

    rows = pieces[0].shape[0]
    copies = [
        pltpu.make_async_copy(piece, held.at[i // parts, pl.ds(i % parts * rows, rows)], piece_sems.at[i])
        for i, piece in enumerate(pieces)
    ]
    for e in range(count):
        for side in range(sides):
            for block in blocks:

                @pl.when(order_ref[e] // per_block == block)
                def _():
                    load(e, side, block).start()

        for copy in copies[e * parts : (e + 1) * parts]:
            copy.start()
    for e in range(count):
        for side in range(sides):
            load(e, side, 0).wait()
        for copy in copies[e * parts : (e + 1) * parts]:
            copy.wait()
        part = jnp.dot(held[e], weights[e], preferred_element_type=jnp.float32)
        if e == 0:
            total[...] = part
        elif e < count - 1:
            total[...] += part
        else:
            out_ref[...] = (total[...] + part).astype(out_ref.dtype)


def product(pieces, sources, order, per_block, dtype):
    count, parts = len(pieces), len(pieces[0])
    rows, depth = pieces[0][0].shape
    rows *= parts
    sides = len(sources[0])
    cols = sides * sources[0][0].shape[2]
    sources = [part for block in sources for part in block]
    in_hbm = pl.BlockSpec(memory_space=pl.ANY)
    return pl.pallas_call(
        functools.partial(product_kernel, count, parts, per_block),
        in_specs=[pl.BlockSpec(memory_space=pltpu.SMEM)] + [in_hbm] * (count * parts + len(sources)),
        out_specs=pl.BlockSpec(memory_space=pltpu.VMEM),
        out_shape=jax.ShapeDtypeStruct((rows, cols), dtype),
        scratch_shapes=[
            pltpu.VMEM((count, rows, depth), jnp.bfloat16),
            pltpu.VMEM((count, depth, cols), jnp.bfloat16),
            pltpu.VMEM((rows, cols), jnp.float32),
            pltpu.SemaphoreType.DMA((count * parts,)),
            pltpu.SemaphoreType.DMA((count, sides)),
        ],
        compiler_params=pltpu.CompilerParams(vmem_limit_bytes=VMEM * MIB),
        cost_estimate=NO_COST,
    )(order, *[part for piece in pieces for part in piece], *sources)


def turn_kernel(panel_ref, out_ref):
    out_ref[...] = jnp.transpose(panel_ref[...], (1, 2, 0))


def turn(panel, first, rows):
    _, tile, near_l = panel.shape
    tall = tile // GROUPS
    wide = min(rows, 128)
    return pl.pallas_call(
        turn_kernel,
        grid=(rows // wide, tile // tall),
        in_specs=[pl.BlockSpec((wide, tall, near_l), lambda i, g: (first // wide + i, g, 0))],
        out_specs=pl.BlockSpec((tall, near_l, wide), lambda i, g: (g, 0, i)),
        out_shape=jax.ShapeDtypeStruct((tile, near_l, rows), panel.dtype),
        compiler_params=pltpu.CompilerParams(vmem_limit_bytes=VMEM * MIB),
        cost_estimate=pl.CostEstimate(flops=0, bytes_accessed=8 * rows * tile * near_l, transcendentals=0),
    )(panel)


def contract_kernel(rb, ab, places_ref, mask_ref, screened_ref, *refs):
    count = places_ref.shape[1]
    held, masked, sems = refs[-3:]
    panels, outs = refs[: -3 - 2 * count], refs[-3 - 2 * count : -3]
    _, tall, share, rows = held.shape
    per_share = masked.shape[1]
    each = rows // len(panels)
    half = outs[0].shape[0]
    steps = [(h, i, g) for h in range(2) for i in range(count) for g in range(half // tall)]

    def load(k):
        h, i, g = steps[k]
        at = pl.ds(pl.multiple_of(places_ref[h, i] * share, share), share)
        return [
            pltpu.make_async_copy(
                panel.at[pl.ds(h * half + g * tall, tall), at, :],
                held.at[k % 2, :, :, pl.ds(n * each, each)],
                sems.at[k % 2, n],
            )
            for n, panel in enumerate(panels)
        ]

    for copy in load(0):
        copy.start()
    for k, (h, i, g) in enumerate(steps):
        if k + 1 < len(steps):
            for copy in load(k + 1):
                copy.start()
        if g == 0:
            for b in range(per_share):
                for n in range(rows // rb):
                    part = screened_ref[pl.ds(n * rb, rb), :]
                    flag = mask_ref[n, places_ref[h, i] * per_share + b]
                    masked[i % 2, b, pl.ds(n * rb, rb), :] = jnp.where(flag != 0, part, jnp.zeros_like(part))
        for copy in load(k):
            copy.wait()
        for b in range(per_share):
            block = held[k % 2, :, pl.ds(b * ab, ab), :].reshape(tall * ab, rows)
            part = jnp.dot(block, masked[i % 2, b], preferred_element_type=jnp.float32)
            outs[h * count + i][pl.ds(g * tall, tall), pl.ds(b * ab, ab), :] = part.astype(outs[0].dtype).reshape(
                tall, ab, part.shape[1]
            )


def contract(panels, screened, mask, places, rb, ab, share):
    count = places.shape[1]
    tile, rows = panels[0].shape[0], screened.shape[0]
    tall = tile // GROUPS
    width = screened.shape[1]
    in_smem, in_hbm = pl.BlockSpec(memory_space=pltpu.SMEM), pl.BlockSpec(memory_space=pl.ANY)
    in_vmem = pl.BlockSpec(memory_space=pltpu.VMEM)
    found = pl.pallas_call(
        functools.partial(contract_kernel, rb, ab),
        in_specs=[in_smem, in_smem, in_vmem] + [in_hbm] * len(panels),
        out_specs=[in_vmem] * (2 * count),
        out_shape=[jax.ShapeDtypeStruct((tile // 2, share, width), jnp.bfloat16)] * (2 * count),
        scratch_shapes=[
            pltpu.VMEM((2, tall, share, rows), jnp.bfloat16),
            pltpu.VMEM((2, share // ab, rows, width), jnp.bfloat16),
            pltpu.SemaphoreType.DMA((2, len(panels))),
        ],
        compiler_params=pltpu.CompilerParams(vmem_limit_bytes=VMEM * MIB),
        cost_estimate=NO_COST,
    )(places, mask, screened, *panels)
    return [list(found[:count]), list(found[count:])]


def scatter_sum(value, axis):
    at = lax.axis_index(axis)
    for bit in bits_below(lax.axis_size(axis)):
        halves = value.reshape(2, value.shape[0] // 2, *value.shape[1:])
        mine = (at // bit) % 2
        value = lax.dynamic_index_in_dim(halves, mine, 0, keepdims=False) + swap(
            lax.dynamic_index_in_dim(halves, 1 - mine, 0, keepdims=False), axis, bit
        )
    return value


def per_device(
    polarization, metric, three_panel, three_near, green_function, mask_panel, mask_near
):
    r, c = lax.axis_index("row"), lax.axis_index("col")
    row_count, col_count = lax.axis_size("row"), lax.axis_size("col")
    top_row, top_col = row_count // 2, col_count // 2
    u, v = r // top_row, c // top_col
    r_low, c_low = r % top_row, c % top_col
    panel_rows, depth = polarization.shape
    near_cols = metric.shape[1]
    half = depth // 2
    per_block = metric.shape[0] // depth
    tile, near_l = three_panel.shape[1], three_panel.shape[2]
    share = near_l // row_count
    width = min(WIDTH, near_cols)
    chunks = near_cols // width
    on_diagonal = u == v

    mine = lax.dynamic_slice_in_dim(polarization, u * half, half, 1)
    other = lax.dynamic_slice_in_dim(polarization, (1 - u) * half, half, 1)
    first, second = jnp.split(mine, 2)
    other_first, other_second = jnp.split(other, 2)
    metric_parts = metric.reshape(per_block, 2, half, near_cols)
    metric_mine = lax.dynamic_index_in_dim(metric_parts, u, 1, keepdims=False)
    metric_other = lax.dynamic_index_in_dim(metric_parts, 1 - u, 1, keepdims=False)
    crossing = [metric_other[:, :, j * width : (j + 1) * width] for j in range(chunks)]

    rb = panel_rows * row_count // mask_panel.shape[0]
    ab = near_l // mask_panel.shape[1]
    row_blocks = panel_rows // rb
    panel_mask = lax.dynamic_slice_in_dim(mask_panel, r * row_blocks, row_blocks, 0)

    low = top_col // 2

    def cross(value, *others):
        return swap(after(value, *others), "row", top_row)

    arrived, came = [cross(crossing[0])], []
    near_first = swap(first, "col", low)
    crossed_first = cross(other_first, arrived[0])
    near_second = swap(after(second, near_first, arrived[0]), "col", low)
    panels = []

    def turn_next(*others):
        rows = panel_rows // GROUPS
        panels.append(turn(after(three_panel, *others), len(panels) * rows, rows))
        return panels[-1]

    def far(j, *others):
        kept = after(metric_mine, arrived[j])[:, :, j * width : (j + 1) * width]
        stay = jnp.where(on_diagonal, kept, arrived[j])
        leave = jnp.where(on_diagonal, arrived[j], kept)
        came.append([stay, swap(after(leave, *others), "col", top_col)])
        return leave

    row_links = {bit: Link(2) for bit in bits_below(top_row)}

    def gather_rows(pair):
        found = {0: pair}
        for bit in bits_below(top_row):
            for f, parts in list(found.items()):
                found[f ^ bit] = [row_links[bit].swap(p, "row", bit) for p in parts]
        return [found[f] for f in range(top_row)]

    row_links = {bit: Link(2) for bit in bits_below(top_row)}
    gathered = []

    def gather_rows(pair):
        found = {0: pair}
        for bit in bits_below(top_row):
            for f, parts in list(found.items()):
                found[f ^ bit] = [row_links[bit].swap(p, "row", bit) for p in parts]
        gathered.append([found[f] for f in range(top_row)])

    def from_row(j, side):
        return gathered[j][-1][side]

    far(0)
    gather_rows(came[0])
    turn_next(near_first)
    arrived.append(cross(crossing[1], arrived[0], near_first))
    crossed_second = cross(other_second, crossed_first, *panels)
    leave = far(1, near_first)
    gather_rows(came[1])
    turn_next(leave, *panels)
    near_crossed_first = swap(after(crossed_first, near_second, arrived[1], came[0][1], from_row(0, 0)), "col", low)
    for j in range(2, chunks):
        due = [came[j - 2][1], near_second, from_row(0, 1), from_row(1, 0)]
        if j == 2:
            arrived.append(cross(crossing[j], arrived[1], *panels))
        else:
            due.append(near_crossed_first)
            while len(panels) < GROUPS:
                turn_next(near_second, came[0][1], from_row(0, 0), *panels)
            arrived.append(cross(crossing[j], crossed_second, *panels))
        leave = far(j, *due)
    while len(panels) < GROUPS:
        turn_next(near_second, *panels)

    near_blocks = near_cols // rb
    near_mask = lax.dynamic_slice_in_dim(mask_near, c * near_blocks, near_blocks, 0)
    near_mask = jnp.repeat(jnp.repeat(near_mask, rb, 0), ab, 1).astype(jnp.bfloat16)
    near = after(three_near, near_crossed_first, came[1][1]) * near_mask[:, None, :]
    green = lax.dynamic_slice_in_dim(green_function, r * share, share, 0)
    dressed = jnp.einsum("qns,ls->nlq", near, green, preferred_element_type=jnp.float32).astype(jnp.bfloat16)

    near_crossed_second = swap(
        after(crossed_second, near_crossed_first, arrived[-1], came[1][1], from_row(0, 1)), "col", low
    )
    near_crossed_second = after(near_crossed_second, dressed, *panels, *[pair[1] for pair in came[2:3]])

    def gather_low(found):
        link = Link(1)
        for bit in bits_below(low):
            for e, parts in list(found.items()):
                found[e ^ bit] = [link.swap(p, "col", bit) if bit > 1 else swap(p, "col", bit) for p in parts]
        return [found[e] for e in range(top_col)]

    pieces_mine = gather_low({0: [first, second], low: [near_first, near_second]})
    pieces_crossed = gather_low({0: [crossed_first, crossed_second], low: [near_crossed_first, near_crossed_second]})
    blocks = c_low ^ jnp.arange(top_col, dtype=jnp.int32)
    order = ((blocks // per_block) ^ r_low) * per_block + blocks % per_block

    screened_chunks, contracted_chunks = [], []
    energy = jnp.zeros((tile, tile), jnp.float32)
    hops = {bit: Link(2) for bit in bits_below(row_count)}
    pair = min(PAIR, chunks)
    wide = pair * width
    orders = [bits_below(row_count)[::-1], bits_below(row_count)]
    kept = [[e for e in range(row_count) if not e & bits[0]] for bits in orders]
    places = r ^ jnp.array(kept, jnp.int32)
    first_bits = jnp.array([[bits[0]] for bits in orders], jnp.int32)
    pairs = chunks // pair

    def sources_of(k):
        at = range(k * pair, (k + 1) * pair)
        return [[gathered[i][f][side] for side in range(2) for i in at] for f in range(top_row)]

    def gather_next(upto, ready):
        for i in range(len(gathered), min(upto, chunks)):
            gather_rows([after(part, ready) for part in came[i]])

    gather_next(pair + 1, pieces_crossed[-1][-1])
    away = product(pieces_crossed, sources_of(0), after(order, leave), per_block, jnp.bfloat16)
    home = product(pieces_mine, sources_of(0), after(order, away), per_block, jnp.float32)
    crossing_back = swap(away, "row", top_row)
    due = [part[1] for part in came[3:4]]
    for k in range(pairs):
        total = after(home, *due) + crossing_back.astype(jnp.float32)
        came_back = swap(total[:, wide:].astype(jnp.bfloat16), "col", top_col)
        if k + 1 < pairs:
            gather_next((k + 2) * pair, away)
            away = product(pieces_crossed, sources_of(k + 1), after(order, home), per_block, jnp.bfloat16)
            crossing_back = swap(away, "row", top_row)
            came_back = after(came_back, away)
        screened = (total[:, :wide] + came_back.astype(jnp.float32)).astype(jnp.bfloat16)
        screened_chunks.append(screened)
        gone = contract(panels, screened, panel_mask, after(places ^ first_bits, away), rb, ab, share)
        if k + 1 < pairs:
            home = product(pieces_mine, sources_of(k + 1), after(order, away, gone, crossing_back), per_block, jnp.float32)
            gone[1] = [after(value, crossing_back) for value in gone[1]]
        stay = contract(panels, screened, panel_mask, after(places, home, gone), rb, ab, share)
        due = []
        left = [[dict(zip(kept[h], part[h])) for part in (gone, stay)] for h in range(2)]
        for hop in range(len(orders[0])):
            for h, bits in enumerate(orders):
                going, staying = left[h]
                next_bit = bits[hop + 1] if hop + 1 < len(bits) else 0
                total = {}
                for e in sorted(going, key=lambda e: -(e & next_bit)):
                    value = hops[bits[hop]].swap(going[e], "row", bits[hop])
                    due += [value] if not hop and not h and e & next_bit else []
                    total[e] = (staying[e].astype(jnp.float32) + value.astype(jnp.float32)).astype(jnp.bfloat16)
                left[h] = [
                    {e & ~next_bit: value for e, value in total.items() if e & next_bit},
                    {e: value for e, value in total.items() if not e & next_bit},
                ]
        halves = [left[h][1][0] for h in range(2)]
        contracted_chunks.append(halves)

    for j, halves in enumerate(contracted_chunks):
        beside = dressed[:, :, j * wide : (j + 1) * wide]
        energy = energy - jnp.concatenate(
            [jnp.einsum("mlq,nlq->mn", half, beside, preferred_element_type=jnp.float32) for half in halves]
        )
    contracted = jnp.transpose(jnp.concatenate([jnp.concatenate(halves) for halves in contracted_chunks], axis=2), (2, 0, 1))
    energy = scatter_sum(after(scatter_sum(energy, "row"), contracted).T, "col").T
    return jnp.concatenate(screened_chunks, axis=1), contracted, energy


def solution(mesh):
    placed = (
        P("row", "col"),
        P("row", "col"),
        P("row", None, None),
        P("col", None, None),
        P(),
        P(),
        P(),
    )
    return jax.shard_map(
        per_device,
        mesh=mesh,
        in_specs=placed,
        out_specs=(P("row", "col"), P("col", None, "row"), P("row", "col")),
        check_vma=False,
    )
```

```python
import functools

import jax
import jax.numpy as jnp
from jax import lax
from jax.experimental import pallas as pl
from jax.experimental.pallas import tpu as pltpu
from jax.sharding import PartitionSpec as P

WIDTH = 128
PAIR = 2
GROUPS = 4
VMEM = 56
NO_COST = pl.CostEstimate(flops=0, bytes_accessed=0, transcendentals=0)
MIB = 1024 * 1024


def swap(value, axis, bit):
    size = lax.axis_size(axis)
    return lax.ppermute(value, axis, [(i, i ^ bit) for i in range(size)])


def after(value, *others):
    return lax.optimization_barrier((value, others))[0]


class Link:
    def __init__(self, in_flight):
        self.past, self.in_flight = [], in_flight

    def swap(self, value, axis, bit):
        if len(self.past) >= self.in_flight:
            value = after(value, self.past[-self.in_flight])
        self.past.append(swap(value, axis, bit))
        return self.past[-1]


def bits_below(size):
    found = []
    while size > 1:
        size //= 2
        found.append(size)
    return found


def product_kernel(count, parts, per_block, order_ref, *refs):
    pieces, sources, out_ref = refs[: count * parts], refs[count * parts : -6], refs[-6]
    held, weights, total, piece_sems, weight_sems = refs[-5:]
    width = sources[0].shape[2]
    sides = weights.shape[2] // width
    blocks = range(len(sources) // sides)

    def load(e, side, block):
        return pltpu.make_async_copy(
            sources[sides * block + side].at[order_ref[e] % per_block],
            weights.at[e, :, pl.ds(side * width, width)],
            weight_sems.at[e, side],
        )

    rows = pieces[0].shape[0]
    copies = [
        pltpu.make_async_copy(piece, held.at[i // parts, pl.ds(i % parts * rows, rows)], piece_sems.at[i])
        for i, piece in enumerate(pieces)
    ]
    for e in range(count):
        for side in range(sides):
            for block in blocks:

                @pl.when(order_ref[e] // per_block == block)
                def _():
                    load(e, side, block).start()

        for copy in copies[e * parts : (e + 1) * parts]:
            copy.start()
    for e in range(count):
        for side in range(sides):
            load(e, side, 0).wait()
        for copy in copies[e * parts : (e + 1) * parts]:
            copy.wait()
        part = jnp.dot(held[e], weights[e], preferred_element_type=jnp.float32)
        if e == 0:
            total[...] = part
        elif e < count - 1:
            total[...] += part
        else:
            out_ref[...] = (total[...] + part).astype(out_ref.dtype)


def product(pieces, sources, order, per_block, dtype):
    count, parts = len(pieces), len(pieces[0])
    rows, depth = pieces[0][0].shape
    rows *= parts
    sides = len(sources[0])
    cols = sides * sources[0][0].shape[2]
    sources = [part for block in sources for part in block]
    in_hbm = pl.BlockSpec(memory_space=pl.ANY)
    return pl.pallas_call(
        functools.partial(product_kernel, count, parts, per_block),
        in_specs=[pl.BlockSpec(memory_space=pltpu.SMEM)] + [in_hbm] * (count * parts + len(sources)),
        out_specs=pl.BlockSpec(memory_space=pltpu.VMEM),
        out_shape=jax.ShapeDtypeStruct((rows, cols), dtype),
        scratch_shapes=[
            pltpu.VMEM((count, rows, depth), jnp.bfloat16),
            pltpu.VMEM((count, depth, cols), jnp.bfloat16),
            pltpu.VMEM((rows, cols), jnp.float32),
            pltpu.SemaphoreType.DMA((count * parts,)),
            pltpu.SemaphoreType.DMA((count, sides)),
        ],
        compiler_params=pltpu.CompilerParams(vmem_limit_bytes=VMEM * MIB),
        cost_estimate=NO_COST,
    )(order, *[part for piece in pieces for part in piece], *sources)


def turn_kernel(panel_ref, out_ref):
    out_ref[...] = jnp.transpose(panel_ref[...], (1, 2, 0))


def turn(panel, first, rows):
    _, tile, near_l = panel.shape
    tall = tile // GROUPS
    wide = min(rows, 128)
    return pl.pallas_call(
        turn_kernel,
        grid=(rows // wide, tile // tall),
        in_specs=[pl.BlockSpec((wide, tall, near_l), lambda i, g: (first // wide + i, g, 0))],
        out_specs=pl.BlockSpec((tall, near_l, wide), lambda i, g: (g, 0, i)),
        out_shape=jax.ShapeDtypeStruct((tile, near_l, rows), panel.dtype),
        compiler_params=pltpu.CompilerParams(vmem_limit_bytes=VMEM * MIB),
        cost_estimate=pl.CostEstimate(flops=0, bytes_accessed=8 * rows * tile * near_l, transcendentals=0),
    )(panel)


def contract_kernel(rb, ab, places_ref, mask_ref, screened_ref, *refs):
    count = places_ref.shape[1]
    held, masked, sems = refs[-3:]
    panels, outs = refs[: -3 - 2 * count], refs[-3 - 2 * count : -3]
    _, tall, share, rows = held.shape
    per_share = masked.shape[1]
    each = rows // len(panels)
    half = outs[0].shape[0]
    steps = [(h, i, g) for h in range(2) for i in range(count) for g in range(half // tall)]

    def load(k):
        h, i, g = steps[k]
        at = pl.ds(pl.multiple_of(places_ref[h, i] * share, share), share)
        return [
            pltpu.make_async_copy(
                panel.at[pl.ds(h * half + g * tall, tall), at, :],
                held.at[k % 2, :, :, pl.ds(n * each, each)],
                sems.at[k % 2, n],
            )
            for n, panel in enumerate(panels)
        ]

    for copy in load(0):
        copy.start()
    for k, (h, i, g) in enumerate(steps):
        if k + 1 < len(steps):
            for copy in load(k + 1):
                copy.start()
        if g == 0:
            for b in range(per_share):
                for n in range(rows // rb):
                    part = screened_ref[pl.ds(n * rb, rb), :]
                    flag = mask_ref[n, places_ref[h, i] * per_share + b]
                    masked[i % 2, b, pl.ds(n * rb, rb), :] = jnp.where(flag != 0, part, jnp.zeros_like(part))
        for copy in load(k):
            copy.wait()
        for b in range(per_share):
            block = held[k % 2, :, pl.ds(b * ab, ab), :].reshape(tall * ab, rows)
            part = jnp.dot(block, masked[i % 2, b], preferred_element_type=jnp.float32)
            outs[h * count + i][pl.ds(g * tall, tall), pl.ds(b * ab, ab), :] = part.astype(outs[0].dtype).reshape(
                tall, ab, part.shape[1]
            )


def contract(panels, screened, mask, places, rb, ab, share):
    count = places.shape[1]
    tile, rows = panels[0].shape[0], screened.shape[0]
    tall = tile // GROUPS
    width = screened.shape[1]
    in_smem, in_hbm = pl.BlockSpec(memory_space=pltpu.SMEM), pl.BlockSpec(memory_space=pl.ANY)
    in_vmem = pl.BlockSpec(memory_space=pltpu.VMEM)
    found = pl.pallas_call(
        functools.partial(contract_kernel, rb, ab),
        in_specs=[in_smem, in_smem, in_vmem] + [in_hbm] * len(panels),
        out_specs=[in_vmem] * (2 * count),
        out_shape=[jax.ShapeDtypeStruct((tile // 2, share, width), jnp.bfloat16)] * (2 * count),
        scratch_shapes=[
            pltpu.VMEM((2, tall, share, rows), jnp.bfloat16),
            pltpu.VMEM((2, share // ab, rows, width), jnp.bfloat16),
            pltpu.SemaphoreType.DMA((2, len(panels))),
        ],
        compiler_params=pltpu.CompilerParams(vmem_limit_bytes=VMEM * MIB),
        cost_estimate=NO_COST,
    )(places, mask, screened, *panels)
    return [list(found[:count]), list(found[count:])]


def scatter_sum(value, axis):
    at = lax.axis_index(axis)
    for bit in bits_below(lax.axis_size(axis)):
        halves = value.reshape(2, value.shape[0] // 2, *value.shape[1:])
        mine = (at // bit) % 2
        value = lax.dynamic_index_in_dim(halves, mine, 0, keepdims=False) + swap(
            lax.dynamic_index_in_dim(halves, 1 - mine, 0, keepdims=False), axis, bit
        )
    return value


def per_device(
    polarization, metric, three_panel, three_near, green_function, mask_panel, mask_near
):
    r, c = lax.axis_index("row"), lax.axis_index("col")
    row_count, col_count = lax.axis_size("row"), lax.axis_size("col")
    top_row, top_col = row_count // 2, col_count // 2
    u, v = r // top_row, c // top_col
    r_low, c_low = r % top_row, c % top_col
    panel_rows, depth = polarization.shape
    near_cols = metric.shape[1]
    half = depth // 2
    per_block = metric.shape[0] // depth
    tile, near_l = three_panel.shape[1], three_panel.shape[2]
    share = near_l // row_count
    width = min(WIDTH, near_cols)
    chunks = near_cols // width
    on_diagonal = u == v

    mine = lax.dynamic_slice_in_dim(polarization, u * half, half, 1)
    other = lax.dynamic_slice_in_dim(polarization, (1 - u) * half, half, 1)
    first, second = jnp.split(mine, 2)
    other_first, other_second = jnp.split(other, 2)
    metric_parts = metric.reshape(per_block, 2, half, near_cols)
    metric_mine = lax.dynamic_index_in_dim(metric_parts, u, 1, keepdims=False)
    metric_other = lax.dynamic_index_in_dim(metric_parts, 1 - u, 1, keepdims=False)
    crossing = [metric_other[:, :, j * width : (j + 1) * width] for j in range(chunks)]

    rb = panel_rows * row_count // mask_panel.shape[0]
    ab = near_l // mask_panel.shape[1]
    row_blocks = panel_rows // rb
    panel_mask = lax.dynamic_slice_in_dim(mask_panel, r * row_blocks, row_blocks, 0)

    low = top_col // 2

    def cross(value, *others):
        return swap(after(value, *others), "row", top_row)

    arrived, came = [cross(crossing[0])], []
    near_first = swap(first, "col", low)
    crossed_first = cross(other_first, arrived[0])
    near_second = swap(after(second, near_first, arrived[0]), "col", low)
    panels = []

    def turn_next(*others):
        rows = panel_rows // GROUPS
        panels.append(turn(after(three_panel, *others), len(panels) * rows, rows))
        return panels[-1]

    def far(j, *others):
        kept = after(metric_mine, arrived[j])[:, :, j * width : (j + 1) * width]
        stay = jnp.where(on_diagonal, kept, arrived[j])
        leave = jnp.where(on_diagonal, arrived[j], kept)
        came.append([stay, swap(after(leave, *others), "col", top_col)])
        return leave

    row_links = {bit: Link(2) for bit in bits_below(top_row)}

    def gather_rows(pair):
        found = {0: pair}
        for bit in bits_below(top_row):
            for f, parts in list(found.items()):
                found[f ^ bit] = [row_links[bit].swap(p, "row", bit) for p in parts]
        return [found[f] for f in range(top_row)]

    row_links = {bit: Link(2) for bit in bits_below(top_row)}
    gathered, stays = [], []

    def rows_of(pair):
        found = {0: pair}
        for bit in bits_below(top_row):
            for f, parts in list(found.items()):
                found[f ^ bit] = [row_links[bit].swap(p, "row", bit) for p in parts]
        return [found[f] for f in range(top_row)]

    def gather_rows(pair):
        gathered.append(rows_of(pair))

    def from_row(j, side):
        return gathered[j][-1][side]

    far(0)
    gather_rows(came[0])
    turn_next(near_first)
    arrived.append(cross(crossing[1], arrived[0], near_first))
    crossed_second = cross(other_second, crossed_first, *panels)
    leave = far(1, near_first)
    gather_rows(came[1])
    turn_next(leave, *panels)
    near_crossed_first = swap(after(crossed_first, near_second, arrived[1], came[0][1], from_row(0, 0)), "col", low)
    for j in range(2, chunks):
        due = [came[j - 2][1], near_second, from_row(0, 1), from_row(1, 0)]
        if j == 2:
            arrived.append(cross(crossing[j], arrived[1], *panels))
        else:
            due.append(near_crossed_first)
            while len(panels) < GROUPS:
                turn_next(near_second, came[0][1], from_row(0, 0), *panels)
            arrived.append(cross(crossing[j], crossed_second, *panels))
        leave = far(j, *due)
        stays.append(rows_of([after(came[j][0], from_row(1, 1))]))
    while len(panels) < GROUPS:
        turn_next(near_second, *panels)

    near_blocks = near_cols // rb
    near_mask = lax.dynamic_slice_in_dim(mask_near, c * near_blocks, near_blocks, 0)
    near_mask = jnp.repeat(jnp.repeat(near_mask, rb, 0), ab, 1).astype(jnp.bfloat16)
    near = after(three_near, near_crossed_first, came[1][1]) * near_mask[:, None, :]
    early = [blocks[-1][0] for blocks in stays]
    green = lax.dynamic_slice_in_dim(after(green_function, *early[:1]), r * share, share, 0)
    dressed = jnp.einsum("qns,ls->nlq", near, green, preferred_element_type=jnp.float32).astype(jnp.bfloat16)

    near_crossed_second = swap(
        after(crossed_second, near_crossed_first, arrived[-1], came[1][1], from_row(0, 1)), "col", low
    )
    near_crossed_second = after(near_crossed_second, dressed, *panels, *early, *[pair[1] for pair in came[2:3]])

    def gather_low(found):
        link = Link(1)
        for bit in bits_below(low):
            for e, parts in list(found.items()):
                found[e ^ bit] = [link.swap(p, "col", bit) if bit > 1 else swap(p, "col", bit) for p in parts]
        return [found[e] for e in range(top_col)]

    pieces_mine = gather_low({0: [first, second], low: [near_first, near_second]})
    pieces_crossed = gather_low({0: [crossed_first, crossed_second], low: [near_crossed_first, near_crossed_second]})
    blocks = c_low ^ jnp.arange(top_col, dtype=jnp.int32)
    order = ((blocks // per_block) ^ r_low) * per_block + blocks % per_block

    screened_chunks, contracted_chunks = [], []
    energy = jnp.zeros((tile, tile), jnp.float32)
    hops = {bit: Link(2) for bit in bits_below(row_count)}
    pair = min(PAIR, chunks)
    wide = pair * width
    orders = [bits_below(row_count)[::-1], bits_below(row_count)]
    kept = [[e for e in range(row_count) if not e & bits[0]] for bits in orders]
    places = r ^ jnp.array(kept, jnp.int32)
    first_bits = jnp.array([[bits[0]] for bits in orders], jnp.int32)
    pairs = chunks // pair

    def sources_of(k):
        at = range(k * pair, (k + 1) * pair)
        return [[gathered[i][f][side] for side in range(2) for i in at] for f in range(top_row)]

    def gather_next(upto, ready):
        for i in range(len(gathered), min(upto, chunks)):
            later = rows_of([after(came[i][1], ready)])
            gathered.append([a + b for a, b in zip(stays[i - 2], later)])

    gather_next(pair + 1, pieces_crossed[-1][-1])
    away = product(pieces_crossed, sources_of(0), after(order, leave), per_block, jnp.bfloat16)
    home = product(pieces_mine, sources_of(0), after(order, away), per_block, jnp.float32)
    crossing_back = swap(away, "row", top_row)
    due = [part[1] for part in came[3:4]]
    for k in range(pairs):
        total = after(home, *due) + crossing_back.astype(jnp.float32)
        came_back = swap(total[:, wide:].astype(jnp.bfloat16), "col", top_col)
        if k + 1 < pairs:
            gather_next((k + 2) * pair, away)
            away = product(pieces_crossed, sources_of(k + 1), after(order, home), per_block, jnp.bfloat16)
            crossing_back = swap(away, "row", top_row)
            came_back = after(came_back, away)
        screened = (total[:, :wide] + came_back.astype(jnp.float32)).astype(jnp.bfloat16)
        screened_chunks.append(screened)
        gone = contract(panels, screened, panel_mask, after(places ^ first_bits, away), rb, ab, share)
        if k + 1 < pairs:
            home = product(pieces_mine, sources_of(k + 1), after(order, away, gone, crossing_back), per_block, jnp.float32)
            gone[1] = [after(value, crossing_back) for value in gone[1]]
        stay = contract(panels, screened, panel_mask, after(places, home, gone), rb, ab, share)
        due = []
        left = [[dict(zip(kept[h], part[h])) for part in (gone, stay)] for h in range(2)]
        for hop in range(len(orders[0])):
            for h, bits in enumerate(orders):
                going, staying = left[h]
                next_bit = bits[hop + 1] if hop + 1 < len(bits) else 0
                total = {}
                for e in sorted(going, key=lambda e: -(e & next_bit)):
                    value = hops[bits[hop]].swap(going[e], "row", bits[hop])
                    due += [value] if not hop and not h and e & next_bit else []
                    total[e] = (staying[e].astype(jnp.float32) + value.astype(jnp.float32)).astype(jnp.bfloat16)
                left[h] = [
                    {e & ~next_bit: value for e, value in total.items() if e & next_bit},
                    {e: value for e, value in total.items() if not e & next_bit},
                ]
        halves = [left[h][1][0] for h in range(2)]
        contracted_chunks.append(halves)

    for j, (front, back) in enumerate(contracted_chunks):
        beside = dressed[:, :, j * wide : (j + 1) * wide]
        of_back = jnp.einsum("mlq,nlq->mn", back, beside, preferred_element_type=jnp.float32)
        of_front = jnp.einsum("mlq,nlq->mn", after(front, of_back), beside, preferred_element_type=jnp.float32)
        energy = energy - jnp.concatenate([of_front, of_back])

    contracted = jnp.transpose(jnp.concatenate([jnp.concatenate(halves) for halves in contracted_chunks], axis=2), (2, 0, 1))
    energy = scatter_sum(after(scatter_sum(energy, "row"), contracted).T, "col").T
    return jnp.concatenate(screened_chunks, axis=1), contracted, energy


def solution(mesh):
    placed = (
        P("row", "col"),
        P("row", "col"),
        P("row", None, None),
        P("col", None, None),
        P(),
        P(),
        P(),
    )
    return jax.shard_map(
        per_device,
        mesh=mesh,
        in_specs=placed,
        out_specs=(P("row", "col"), P("col", None, "row"), P("row", "col")),
        check_vma=False,
    )
```

```python
import functools

import jax
import jax.numpy as jnp
from jax import lax
from jax.experimental import pallas as pl
from jax.experimental.pallas import tpu as pltpu
from jax.sharding import PartitionSpec as P

WIDTH = 128
PAIR = 2
GROUPS = 4
VMEM = 56
NO_COST = pl.CostEstimate(flops=0, bytes_accessed=0, transcendentals=0)
MIB = 1024 * 1024


def swap(value, axis, bit):
    size = lax.axis_size(axis)
    return lax.ppermute(value, axis, [(i, i ^ bit) for i in range(size)])


def after(value, *others):
    return lax.optimization_barrier((value, others))[0]


class Link:
    def __init__(self, in_flight):
        self.past, self.in_flight = [], in_flight

    def swap(self, value, axis, bit):
        if len(self.past) >= self.in_flight:
            value = after(value, self.past[-self.in_flight])
        self.past.append(swap(value, axis, bit))
        return self.past[-1]


def bits_below(size):
    found = []
    while size > 1:
        size //= 2
        found.append(size)
    return found


def product_kernel(count, parts, per_block, order_ref, *refs):
    pieces, sources, out_ref = refs[: count * parts], refs[count * parts : -6], refs[-6]
    held, weights, total, piece_sems, weight_sems = refs[-5:]
    width = sources[0].shape[2]
    sides = weights.shape[2] // width
    blocks = range(len(sources) // sides)

    def load(e, side, block):
        return pltpu.make_async_copy(
            sources[sides * block + side].at[order_ref[e] % per_block],
            weights.at[e, :, pl.ds(side * width, width)],
            weight_sems.at[e, side],
        )

    rows = pieces[0].shape[0]
    copies = [
        pltpu.make_async_copy(piece, held.at[i // parts, pl.ds(i % parts * rows, rows)], piece_sems.at[i])
        for i, piece in enumerate(pieces)
    ]
    for e in range(count):
        for side in range(sides):
            for block in blocks:

                @pl.when(order_ref[e] // per_block == block)
                def _():
                    load(e, side, block).start()

        for copy in copies[e * parts : (e + 1) * parts]:
            copy.start()
    for e in range(count):
        for side in range(sides):
            load(e, side, 0).wait()
        for copy in copies[e * parts : (e + 1) * parts]:
            copy.wait()
        part = jnp.dot(held[e], weights[e], preferred_element_type=jnp.float32)
        if e == 0:
            total[...] = part
        elif e < count - 1:
            total[...] += part
        else:
            out_ref[...] = (total[...] + part).astype(out_ref.dtype)


def product(pieces, sources, order, per_block, dtype):
    count, parts = len(pieces), len(pieces[0])
    rows, depth = pieces[0][0].shape
    rows *= parts
    sides = len(sources[0])
    cols = sides * sources[0][0].shape[2]
    sources = [part for block in sources for part in block]
    in_hbm = pl.BlockSpec(memory_space=pl.ANY)
    return pl.pallas_call(
        functools.partial(product_kernel, count, parts, per_block),
        in_specs=[pl.BlockSpec(memory_space=pltpu.SMEM)] + [in_hbm] * (count * parts + len(sources)),
        out_specs=pl.BlockSpec(memory_space=pltpu.VMEM),
        out_shape=jax.ShapeDtypeStruct((rows, cols), dtype),
        scratch_shapes=[
            pltpu.VMEM((count, rows, depth), jnp.bfloat16),
            pltpu.VMEM((count, depth, cols), jnp.bfloat16),
            pltpu.VMEM((rows, cols), jnp.float32),
            pltpu.SemaphoreType.DMA((count * parts,)),
            pltpu.SemaphoreType.DMA((count, sides)),
        ],
        compiler_params=pltpu.CompilerParams(vmem_limit_bytes=VMEM * MIB),
        cost_estimate=NO_COST,
    )(order, *[part for piece in pieces for part in piece], *sources)


def turn_kernel(panel_ref, out_ref):
    out_ref[...] = jnp.transpose(panel_ref[...], (1, 2, 0))


def turn(panel, first, rows):
    _, tile, near_l = panel.shape
    tall = tile // GROUPS
    wide = min(rows, 128)
    return pl.pallas_call(
        turn_kernel,
        grid=(rows // wide, tile // tall),
        in_specs=[pl.BlockSpec((wide, tall, near_l), lambda i, g: (first // wide + i, g, 0))],
        out_specs=pl.BlockSpec((tall, near_l, wide), lambda i, g: (g, 0, i)),
        out_shape=jax.ShapeDtypeStruct((tile, near_l, rows), panel.dtype),
        compiler_params=pltpu.CompilerParams(vmem_limit_bytes=VMEM * MIB),
        cost_estimate=pl.CostEstimate(flops=0, bytes_accessed=8 * rows * tile * near_l, transcendentals=0),
    )(panel)


def contract_kernel(rb, ab, places_ref, mask_ref, screened_ref, *refs):
    count = places_ref.shape[1]
    held, masked, sems = refs[-3:]
    panels, outs = refs[: -3 - 2 * count], refs[-3 - 2 * count : -3]
    _, tall, share, rows = held.shape
    per_share = masked.shape[1]
    each = rows // len(panels)
    half = outs[0].shape[0]
    steps = [(h, i, g) for h in range(2) for i in range(count) for g in range(half // tall)]

    def load(k):
        h, i, g = steps[k]
        at = pl.ds(pl.multiple_of(places_ref[h, i] * share, share), share)
        return [
            pltpu.make_async_copy(
                panel.at[pl.ds(h * half + g * tall, tall), at, :],
                held.at[k % 2, :, :, pl.ds(n * each, each)],
                sems.at[k % 2, n],
            )
            for n, panel in enumerate(panels)
        ]

    for copy in load(0):
        copy.start()
    for k, (h, i, g) in enumerate(steps):
        if k + 1 < len(steps):
            for copy in load(k + 1):
                copy.start()
        if g == 0:
            for b in range(per_share):
                for n in range(rows // rb):
                    part = screened_ref[pl.ds(n * rb, rb), :]
                    flag = mask_ref[n, places_ref[h, i] * per_share + b]
                    masked[i % 2, b, pl.ds(n * rb, rb), :] = jnp.where(flag != 0, part, jnp.zeros_like(part))
        for copy in load(k):
            copy.wait()
        for b in range(per_share):
            block = held[k % 2, :, pl.ds(b * ab, ab), :].reshape(tall * ab, rows)
            part = jnp.dot(block, masked[i % 2, b], preferred_element_type=jnp.float32)
            outs[h * count + i][pl.ds(g * tall, tall), pl.ds(b * ab, ab), :] = part.astype(outs[0].dtype).reshape(
                tall, ab, part.shape[1]
            )


def contract(panels, screened, mask, places, rb, ab, share):
    count = places.shape[1]
    tile, rows = panels[0].shape[0], screened.shape[0]
    tall = tile // GROUPS
    width = screened.shape[1]
    in_smem, in_hbm = pl.BlockSpec(memory_space=pltpu.SMEM), pl.BlockSpec(memory_space=pl.ANY)
    in_vmem = pl.BlockSpec(memory_space=pltpu.VMEM)
    found = pl.pallas_call(
        functools.partial(contract_kernel, rb, ab),
        in_specs=[in_smem, in_smem, in_vmem] + [in_hbm] * len(panels),
        out_specs=[in_vmem] * (2 * count),
        out_shape=[jax.ShapeDtypeStruct((tile // 2, share, width), jnp.bfloat16)] * (2 * count),
        scratch_shapes=[
            pltpu.VMEM((2, tall, share, rows), jnp.bfloat16),
            pltpu.VMEM((2, share // ab, rows, width), jnp.bfloat16),
            pltpu.SemaphoreType.DMA((2, len(panels))),
        ],
        compiler_params=pltpu.CompilerParams(vmem_limit_bytes=VMEM * MIB),
        cost_estimate=NO_COST,
    )(places, mask, screened, *panels)
    return [list(found[:count]), list(found[count:])]


def scatter_sum(value, axis):
    at = lax.axis_index(axis)
    for bit in bits_below(lax.axis_size(axis)):
        halves = value.reshape(2, value.shape[0] // 2, *value.shape[1:])
        mine = (at // bit) % 2
        value = lax.dynamic_index_in_dim(halves, mine, 0, keepdims=False) + swap(
            lax.dynamic_index_in_dim(halves, 1 - mine, 0, keepdims=False), axis, bit
        )
    return value


def per_device(
    polarization, metric, three_panel, three_near, green_function, mask_panel, mask_near
):
    r, c = lax.axis_index("row"), lax.axis_index("col")
    row_count, col_count = lax.axis_size("row"), lax.axis_size("col")
    top_row, top_col = row_count // 2, col_count // 2
    u, v = r // top_row, c // top_col
    r_low, c_low = r % top_row, c % top_col
    panel_rows, depth = polarization.shape
    near_cols = metric.shape[1]
    half = depth // 2
    per_block = metric.shape[0] // depth
    tile, near_l = three_panel.shape[1], three_panel.shape[2]
    share = near_l // row_count
    width = min(WIDTH, near_cols)
    chunks = near_cols // width
    on_diagonal = u == v

    mine = lax.dynamic_slice_in_dim(polarization, u * half, half, 1)
    other = lax.dynamic_slice_in_dim(polarization, (1 - u) * half, half, 1)
    first, second = jnp.split(mine, 2)
    other_first, other_second = jnp.split(other, 2)
    metric_parts = metric.reshape(per_block, 2, half, near_cols)
    metric_mine = lax.dynamic_index_in_dim(metric_parts, u, 1, keepdims=False)
    metric_other = lax.dynamic_index_in_dim(metric_parts, 1 - u, 1, keepdims=False)
    crossing = [metric_other[:, :, j * width : (j + 1) * width] for j in range(chunks)]

    rb = panel_rows * row_count // mask_panel.shape[0]
    ab = near_l // mask_panel.shape[1]
    row_blocks = panel_rows // rb
    panel_mask = lax.dynamic_slice_in_dim(mask_panel, r * row_blocks, row_blocks, 0)

    low = top_col // 2

    def cross(value, *others):
        return swap(after(value, *others), "row", top_row)

    arrived, came = [cross(crossing[0])], []
    near_first = swap(first, "col", low)
    crossed_first = cross(other_first, arrived[0])
    near_second = swap(after(second, near_first, arrived[0]), "col", low)
    panels = []

    def turn_next(*others):
        rows = panel_rows // GROUPS
        panels.append(turn(after(three_panel, *others), len(panels) * rows, rows))
        return panels[-1]

    def far(j, *others):
        kept = after(metric_mine, arrived[j])[:, :, j * width : (j + 1) * width]
        stay = jnp.where(on_diagonal, kept, arrived[j])
        leave = jnp.where(on_diagonal, arrived[j], kept)
        came.append([stay, swap(after(leave, *others), "col", top_col)])
        return leave

    row_links = {bit: Link(2) for bit in bits_below(top_row)}

    def gather_rows(pair):
        found = {0: pair}
        for bit in bits_below(top_row):
            for f, parts in list(found.items()):
                found[f ^ bit] = [row_links[bit].swap(p, "row", bit) for p in parts]
        return [found[f] for f in range(top_row)]

    row_links = {bit: Link(2) for bit in bits_below(top_row)}
    gathered, stays = [], []

    def rows_of(pair):
        found = {0: pair}
        for bit in bits_below(top_row):
            for f, parts in list(found.items()):
                found[f ^ bit] = [row_links[bit].swap(p, "row", bit) for p in parts]
        return [found[f] for f in range(top_row)]

    def gather_rows(pair):
        gathered.append(rows_of(pair))

    def from_row(j, side):
        return gathered[j][-1][side]

    far(0)
    gather_rows(came[0])
    turn_next(near_first)
    arrived.append(cross(crossing[1], arrived[0], near_first))
    crossed_second = cross(other_second, crossed_first, *panels)
    leave = far(1, near_first)
    gather_rows(came[1])
    turn_next(leave, *panels)
    near_crossed_first = swap(after(crossed_first, near_second, arrived[1], came[0][1], from_row(0, 0)), "col", low)
    for j in range(2, chunks):
        due = [came[j - 2][1], near_second, from_row(0, 1), from_row(1, 0)]
        if j == 2:
            arrived.append(cross(crossing[j], arrived[1], *panels))
        else:
            due.append(near_crossed_first)
            while len(panels) < GROUPS:
                turn_next(near_second, came[0][1], from_row(0, 0), *panels)
            arrived.append(cross(crossing[j], crossed_second, *panels))
        leave = far(j, *due)
        stays.append(rows_of([after(came[j][0], from_row(1, 1))]))
    while len(panels) < GROUPS:
        turn_next(near_second, *panels)

    near_blocks = near_cols // rb
    near_mask = lax.dynamic_slice_in_dim(mask_near, c * near_blocks, near_blocks, 0)
    near_mask = jnp.repeat(jnp.repeat(near_mask, rb, 0), ab, 1).astype(jnp.bfloat16)
    near = after(three_near, near_crossed_first, came[1][1]) * near_mask[:, None, :]
    early = [blocks[-1][0] for blocks in stays]
    green = lax.dynamic_slice_in_dim(after(green_function, *early[:1]), r * share, share, 0)
    dressed = jnp.einsum("qns,ls->nlq", near, green, preferred_element_type=jnp.float32).astype(jnp.bfloat16)

    near_crossed_second = swap(
        after(crossed_second, near_crossed_first, arrived[-1], came[1][1], from_row(0, 1)), "col", low
    )
    near_crossed_second = after(near_crossed_second, dressed, *panels, *early, *[pair[1] for pair in came[2:3]])

    def gather_low(found):
        link = Link(1)
        for bit in bits_below(low):
            for e, parts in list(found.items()):
                found[e ^ bit] = [link.swap(p, "col", bit) if bit > 1 else swap(p, "col", bit) for p in parts]
        return [found[e] for e in range(top_col)]

    pieces_mine = gather_low({0: [first, second], low: [near_first, near_second]})
    pieces_crossed = gather_low({0: [crossed_first, crossed_second], low: [near_crossed_first, near_crossed_second]})
    blocks = c_low ^ jnp.arange(top_col, dtype=jnp.int32)
    order = ((blocks // per_block) ^ r_low) * per_block + blocks % per_block

    screened_chunks, contracted_chunks = [], []
    energy = jnp.zeros((tile, tile), jnp.float32)
    hops = {bit: Link(2) for bit in bits_below(row_count)}
    pair = min(PAIR, chunks)
    wide = pair * width
    orders = [bits_below(row_count)[::-1], bits_below(row_count)]
    kept = [[e for e in range(row_count) if not e & bits[0]] for bits in orders]
    places = r ^ jnp.array(kept, jnp.int32)
    first_bits = jnp.array([[bits[0]] for bits in orders], jnp.int32)
    pairs = chunks // pair

    def sources_of(k):
        at = range(k * pair, (k + 1) * pair)
        return [[gathered[i][f][side] for side in range(2) for i in at] for f in range(top_row)]

    def gather_next(upto, ready):
        for i in range(len(gathered), min(upto, chunks)):
            later = rows_of([after(came[i][1], ready)])
            gathered.append([a + b for a, b in zip(stays[i - 2], later)])

    gather_next(pair + 1, pieces_crossed[-1][-1])
    away = product(pieces_crossed, sources_of(0), after(order, leave), per_block, jnp.bfloat16)
    home = product(pieces_mine, sources_of(0), after(order, away), per_block, jnp.float32)
    crossing_back = swap(away, "row", top_row)
    due = [part[1] for part in came[3:4]]
    for k in range(pairs):
        total = after(home, *due) + crossing_back.astype(jnp.float32)
        came_back = swap(total[:, wide:].astype(jnp.bfloat16), "col", top_col)
        if k + 1 < pairs:
            gather_next((k + 2) * pair, away)
            away = product(pieces_crossed, sources_of(k + 1), after(order, home), per_block, jnp.bfloat16)
            crossing_back = swap(away, "row", top_row)
            came_back = after(came_back, away)
        screened = (total[:, :wide] + came_back.astype(jnp.float32)).astype(jnp.bfloat16)
        screened_chunks.append(screened)
        gone = contract(panels, screened, panel_mask, after(places ^ first_bits, away), rb, ab, share)
        if k + 1 < pairs:
            home = product(pieces_mine, sources_of(k + 1), after(order, away, gone, crossing_back), per_block, jnp.float32)
            gone[1] = [after(value, crossing_back) for value in gone[1]]
        stay = contract(panels, screened, panel_mask, after(places, home, gone), rb, ab, share)
        due = []
        left = [[dict(zip(kept[h], part[h])) for part in (gone, stay)] for h in range(2)]
        for hop in range(len(orders[0])):
            for h, bits in enumerate(orders):
                going, staying = left[h]
                next_bit = bits[hop + 1] if hop + 1 < len(bits) else 0
                total = {}
                for e in sorted(going, key=lambda e: -(e & next_bit)):
                    value = hops[bits[hop]].swap(going[e], "row", bits[hop])
                    due += [value] if not hop and not h and e & next_bit else []
                    total[e] = (staying[e].astype(jnp.float32) + value.astype(jnp.float32)).astype(jnp.bfloat16)
                left[h] = [
                    {e & ~next_bit: value for e, value in total.items() if e & next_bit},
                    {e: value for e, value in total.items() if not e & next_bit},
                ]
        halves = [left[h][1][0] for h in range(2)]
        contracted_chunks.append(halves)

    for j, (front, back) in enumerate(contracted_chunks):
        beside = dressed[:, :, j * wide : (j + 1) * wide]
        of_front = jnp.einsum("mlq,nlq->mn", front, beside, preferred_element_type=jnp.float32)
        of_back = jnp.einsum("mlq,nlq->mn", after(back, of_front), beside, preferred_element_type=jnp.float32)
        energy = energy - jnp.concatenate([of_front, of_back])

    contracted = jnp.transpose(jnp.concatenate([jnp.concatenate(halves) for halves in contracted_chunks], axis=2), (2, 0, 1))
    energy = scatter_sum(after(scatter_sum(energy, "row"), contracted).T, "col").T
    return jnp.concatenate(screened_chunks, axis=1), contracted, energy


def solution(mesh):
    placed = (
        P("row", "col"),
        P("row", "col"),
        P("row", None, None),
        P("col", None, None),
        P(),
        P(),
        P(),
    )
    return jax.shard_map(
        per_device,
        mesh=mesh,
        in_specs=placed,
        out_specs=(P("row", "col"), P("col", None, "row"), P("row", "col")),
        check_vma=False,
    )
```
